512 devices in a mesh: slab: 8 (over y), rve: 64 (over x, z, core).
Axes of the slice: x: 4, y: 8, z: 8, core: 2. Of those that a mesh axis runs over, the one named last changes fastest.
Arguments:
- macro_field: float32 [3, 65536], P(None, ('slab', 'rve')), may hold values from -6 to 6
- rve_owner: int32 [65536, 1], P(('slab', 'rve')), may hold values from 0 to 63; in each aligned block of 128 rows (0 to 127, 128 to 255, ...) at most 4 rows name the same one
- potential: float32 [65536, 512], P(('slab', 'rve')), may hold values from -3 to 3
- switch_words: int32 [131072, 512], P(('slab', 'rve')), may hold values from 0 to 15
- permeability: float32 [131072, 512], P(('slab', 'rve')), may hold values from 0.5 to 4
- coercivity: float32 [131072, 512], P(('slab', 'rve')), may hold values from 0.5 to 2
- grain_axes: float32 [3, 131072, 512], P(None, ('slab', 'rve')), may hold values from 0.5 to 2
- hyst_axis: float32 [3, 4], replicated, may hold values from 0.05 to 1
- hyst_low: float32 [4], replicated, may hold values from -1.5 to -0.1
- hyst_high: float32 [4], replicated, may hold values from 0.1 to 1.5
- hyst_weight: float32 [4], replicated, may hold values from 0.2 to 1
- grad_weights: float32 [3, 8, 65536], P(None, None, ('slab', 'rve')), may hold values from -0.3 to 0.3
- connectivity: int32 [8, 65536], P(None, ('slab', 'rve')), may hold values from 0 to 44, as said below
- node_order: int32 [23040], P(('slab', 'rve')), may hold values from 0 to 44, as said below
Outputs:
- potential_new: float32 [65536, 512], P(('slab', 'rve'))
- tangent: float32 [3, 3, 65536], P(None, None, ('slab', 'rve'))
- residual: float32 [23040], P(('slab', 'rve'))
The draws below stay inside these ranges and needn't reach their ends.
Inputs may be any that keep to these rules, and one draw needn't show every extreme that they name: `rve_owner`: owner of a point's RVE along rve, in the point's slab. Among the 128 points of one block at most 4 name the same owner, a bound that some block reaches. `switch_words`: bit k (k below 4) of a voxel's word is hysteron k's last switching state, 1 for up. `connectivity`: A block holds 2 x 2 x 4 hexahedra of 8 points each; the corners of a point's hexahedron, corner a at offsets (a // 4, a // 2 % 2, a % 2), as local node numbers agreeing with node_order. `node_order`: for each block a permutation of the local node numbers, listed by structured position with z fastest.
All inputs are finite; a program needn't handle non-finite values.
Results may differ from the reference program's by a relative error of at most 0.0003.
Values sent between devices are 32-bit elements; how exact they have to be, the bound alone decides.
A program may use at most 64 MiB of HBM per device.

```python
import math
import jax
import jax.numpy as jnp
import numpy as np
from jax import lax

RES = 8
VOX = 512
NHYS = 4
SWEEPS = 2
GAUSS = 8
EX = 2
EY = 2
EZ = 4
Q_DEV = 128
QUADS = 65536
CAP = 4
SLOTS_ALL = 131072
NODES_LOC = 45
NODES = 23040
N_SLAB = 8
N_RVE = 64


def one_order(subkey):
    return jax.random.permutation(subkey, NODES_LOC)


def local_orders(key):
    blocks = QUADS // Q_DEV
    subkeys = jax.random.split(jax.random.fold_in(key, 17), blocks)
    return jax.vmap(one_order)(subkeys).astype(jnp.int32)


def draw_node_order(key, part):
    return local_orders(key).reshape(-1)


def draw_connectivity(key, part):
    orders = local_orders(key)
    points = jnp.arange(Q_DEV, dtype=jnp.int32)
    element = points // GAUSS
    layer_z = element % EZ
    layer_y = element // EZ % EY
    layer_x = element // (EZ * EY)
    corner = jnp.arange(8, dtype=jnp.int32)
    shift_x = corner // 4
    shift_y = corner // 2 % 2
    shift_z = corner % 2
    structured = ((layer_x[None, :] + shift_x[:, None]) * (EY + 1) + layer_y[None, :] + shift_y[:, None]) * (EZ + 1) + layer_z[None, :] + shift_z[:, None]
    picked = orders[:, structured]
    return jnp.transpose(picked, (1, 0, 2)).reshape(8, QUADS).astype(jnp.int32)


def touch_ends(entries, own_key, low, top_value):
    spot = [jax.random.randint(jax.random.fold_in(own_key, axis), (), 0, length) for axis, length in enumerate(entries.shape)]
    longest = entries.shape.index(max(entries.shape))
    next_to = spot[:longest] + [(spot[longest] + 1) % entries.shape[longest]] + spot[longest + 1:]
    return entries.at[tuple(spot)].set(low).at[tuple(next_to)].set(top_value)


def block_scale(own_key, dims, cuts, low, top_value):
    def one(dim, blocks):
        steps = jax.random.uniform(jax.random.fold_in(jax.random.fold_in(own_key, 6), dim), (blocks,), jnp.float32, low / len(cuts), top_value / len(cuts))
        return jnp.repeat(jnp.exp(steps), dims[dim] // blocks).reshape((-1,) + (1,) * (len(dims) - dim - 1))

    loudness = one(*cuts[0])
    for cut in cuts[1:]:
        loudness = loudness * one(*cut)
    return loudness


def assign_block(key, own, number, rows, number_of, top, most, slope):
    order = jax.random.permutation(key, number_of)
    crowded, ordinary = load_shares(number_of, rows * top, most, slope, True), load_shares(number_of, rows * top, most, slope, False)
    places = jnp.arange(number_of)

    def named(lengths, rotation):
        used = int((lengths > 0).sum())
        fixed = max(1, used // 4)
        shifted = fixed + (places - fixed + rotation * (used - fixed)) % max(1, number_of - fixed)
        return jnp.zeros((number_of,), jnp.int32).at[order[jnp.where(places < fixed, places, shifted)]].set(jnp.asarray(lengths, jnp.int32))

    lengths = jnp.where(number % 4 == 0, named(crowded, number // 4), named(ordinary, number - number // 4 - 1))
    mixed = jax.random.permutation(jax.random.fold_in(own, 3), number_of)
    donor, receiver = mixed[0:number_of // 2 * 2:2], mixed[1:number_of // 2 * 2:2]
    slack = jnp.minimum(lengths[donor] - 1, most - lengths[receiver]) // 2
    slack = jnp.where((donor == order[0]) | (receiver == order[0]) | (lengths[receiver] == 0), 0, jnp.maximum(slack, 0))
    shifted = jax.random.randint(jax.random.fold_in(own, 4), (number_of // 2,), 0, 1 << 20) % (slack + 1)
    lengths = lengths.at[donor].add(-shifted).at[receiver].add(shifted)
    labels = jnp.searchsorted(jnp.cumsum(lengths), jnp.arange(rows * top), side="right").astype(jnp.int32)
    listing = labels.reshape(top, rows).T
    listing = listing[jax.random.permutation(jax.random.fold_in(own, 1), rows)]
    rotation = jax.random.randint(jax.random.fold_in(own, 2), (rows, 1), 0, top)
    return jnp.take_along_axis(listing, (jnp.arange(top)[None, :] + rotation) % top, axis=1)


def load_shares(count, total, limit, skew, full):
    portions = [(1 << 20) // math.isqrt(standing ** skew) + 1 for standing in range(1, count + 1)]
    largest = limit if full else min(limit, max(-(-total // count), total * portions[0] // sum(portions)))
    least = 1 if total - largest >= count - 1 else 0
    given, rest = [largest] + [least] * (count - 1), total - largest - least * (count - 1)
    while rest > 0:
        movable = [i for i in range(1, count) if given[i] < largest] or [i for i in range(1, count) if given[i] < limit]
        mass, budget = sum([portions[i] for i in movable]), rest
        for i in movable:
            extra = min(limit - given[i], max(1, budget * portions[i] // mass), rest)
            given[i] = given[i] + extra
            rest = rest - extra
    return np.array(given)


def gaussian(key, extent, scale, bound, cuts=(), held_as=jnp.bfloat16):
    drawn = scale * jax.random.normal(key, extent, jnp.float32)
    if cuts:
        drawn = drawn * block_scale(key, extent, cuts, -0.22, 0.18)
    return jnp.clip(drawn, -bound, bound).astype(held_as)


def setup_inputs(seed: int = 0) -> dict:
    arg_keys = jax.random.split(jax.random.key(seed), 15)
    macro_field = gaussian(arg_keys[0], (3, QUADS), 1.0, 6.0, ((1, 512),), jnp.float32)
    rve_owner_keys = jax.random.split(jax.random.fold_in(arg_keys[1], 1), QUADS // Q_DEV)
    rve_owner_turns = jax.random.permutation(jax.random.fold_in(arg_keys[1], 3), QUADS // Q_DEV)
    rve_owner = jax.vmap(lambda own, number: assign_block(jax.random.fold_in(arg_keys[1], 2), own, number, Q_DEV, N_RVE, 1, CAP, 2))(rve_owner_keys, rve_owner_turns).reshape((QUADS, 1))
    potential = gaussian(arg_keys[2], (QUADS, VOX), 0.5, 3.0, ((0, 512),), jnp.float32)
    switch_words = touch_ends(jax.random.randint(arg_keys[3], (SLOTS_ALL, VOX), 0, 2 ** NHYS), jax.random.fold_in(arg_keys[3], 1), 0, (2 ** NHYS) - 1).astype(jnp.int32)
    permeability = jnp.clip(jnp.exp(math.log(4.0) - 2.0794415 * jax.random.uniform(arg_keys[4], (SLOTS_ALL, VOX), jnp.float32) ** block_scale(arg_keys[4], (SLOTS_ALL, VOX), ((0, 512),), -0.2, 0.2)), 0.5, 4.0)
    coercivity = jnp.clip(jnp.exp(math.log(2.0) - 1.3862944 * jax.random.uniform(arg_keys[5], (SLOTS_ALL, VOX), jnp.float32) ** block_scale(arg_keys[5], (SLOTS_ALL, VOX), ((0, 512),), -0.2, 0.2)), 0.5, 2.0)
    grain_axes = jnp.clip(jnp.exp(math.log(2.0) - 1.3862944 * jax.random.uniform(arg_keys[6], (3, SLOTS_ALL, VOX), jnp.float32) ** block_scale(arg_keys[6], (3, SLOTS_ALL, VOX), ((1, 512),), -0.2, 0.2)), 0.5, 2.0)
    hyst_axis = jnp.clip(jax.random.uniform(arg_keys[7], (3, NHYS), jnp.float32, 0.05, 1.0), 0.05, 1.0)
    hyst_low = jnp.clip(jax.random.uniform(arg_keys[8], (NHYS,), jnp.float32, -1.5, -0.1), -1.5, -0.1)
    hyst_high = jnp.clip(jax.random.uniform(arg_keys[9], (NHYS,), jnp.float32, 0.1, 1.5), 0.1, 1.5)
    hyst_weight = jnp.clip(jnp.exp(jax.random.uniform(arg_keys[10], (NHYS,), jnp.float32, math.log(0.2), math.log(1.0))), 0.2, 1.0)
    grad_weights = gaussian(arg_keys[11], (3, 8, QUADS), 0.05, 0.3, ((2, 512),), jnp.float32)
    connectivity = draw_connectivity(jax.random.fold_in(arg_keys[14], 71), 0)
    node_order = draw_node_order(jax.random.fold_in(arg_keys[14], 71), 0)
    return {"macro_field": macro_field, "rve_owner": rve_owner, "potential": potential, "switch_words": switch_words, "permeability": permeability, "coercivity": coercivity, "grain_axes": grain_axes, "hyst_axis": hyst_axis, "hyst_low": hyst_low, "hyst_high": hyst_high, "hyst_weight": hyst_weight, "grad_weights": grad_weights, "connectivity": connectivity, "node_order": node_order}


slope_gain = 2.0
diag_boost = 1.5


def neighbour(values, stride, forward):
    cell_count = values.shape[-1]
    position = (lax.iota(jnp.int32, cell_count) // stride) % RES
    if forward:
        within = jnp.roll(values, -stride, axis=-1)
        wrapped = jnp.roll(values, (RES - 1) * stride, axis=-1)
        border = position == RES - 1
    else:
        within = jnp.roll(values, stride, axis=-1)
        wrapped = jnp.roll(values, (1 - RES) * stride, axis=-1)
        border = position == 0
    return jnp.where(border, wrapped, within)


def evaluate(potential_now, sensitivity, mean_field, permeability, grain_axes, thresholds, hyst_axis, hyst_weight):
    strides = (RES * RES, RES, 1)
    local_field = [mean_field[component] + neighbour(potential_now, strides[component], True) - potential_now for component in range(3)]
    grain_field = [grain_axes[component] * local_field[component] for component in range(3)]
    magnet_sum = [0.0, 0.0, 0.0]
    pairs = [(0, 0), (0, 1), (0, 2), (1, 1), (1, 2), (2, 2)]
    stiff_sum = {pair: 0.0 for pair in pairs}
    for hysteron in range(NHYS):
        projection = hyst_axis[0, hysteron] * grain_field[0] + hyst_axis[1, hysteron] * grain_field[1] + hyst_axis[2, hysteron] * grain_field[2]
        switch = jnp.tanh(slope_gain * (projection - thresholds[hysteron]))
        slope_now = slope_gain * hyst_weight[hysteron] * (1.0 - switch * switch)
        for component in range(3):
            magnet_sum[component] = magnet_sum[component] + (hyst_weight[hysteron] * hyst_axis[component, hysteron]) * switch
        for pair in pairs:
            stiff_sum[pair] = stiff_sum[pair] + (hyst_axis[pair[0], hysteron] * hyst_axis[pair[1], hysteron]) * slope_now
    micro_flux = [permeability * (local_field[component] + grain_axes[component] * magnet_sum[component]) for component in range(3)]
    tangent_local = [[permeability * (grain_axes[left_comp] * grain_axes[right_comp] * stiff_sum[(min(left_comp, right_comp), max(left_comp, right_comp))] + (1.0 if left_comp == right_comp else 0.0)) for right_comp in range(3)] for left_comp in range(3)]
    gradients = [[neighbour(sensitivity[column], strides[left_comp], True) - sensitivity[column] + (1.0 if left_comp == column else 0.0) for column in range(3)] for left_comp in range(3)]
    linear_flux = [[tangent_local[left_comp][0] * gradients[0][column] + tangent_local[left_comp][1] * gradients[1][column] + tangent_local[left_comp][2] * gradients[2][column] for column in range(3)] for left_comp in range(3)]
    return micro_flux, tangent_local, linear_flux


def divergence(fields):
    strides = (RES * RES, RES, 1)
    summed = fields[0] - neighbour(fields[0], strides[0], False)
    for component in (1, 2):
        summed = summed + fields[component] - neighbour(fields[component], strides[component], False)
    return summed


def micro_solve(potential_now, mean_field, switch_words, permeability, coercivity, grain_axes, hyst_axis, hyst_low, hyst_high, hyst_weight):
    strides = (RES * RES, RES, 1)
    thresholds = [coercivity * jnp.where(jnp.bitwise_and(jnp.right_shift(switch_words, hysteron), 1) == 1, hyst_low[hysteron], hyst_high[hysteron]) for hysteron in range(NHYS)]
    sensitivity = [jnp.zeros_like(potential_now) for component in range(3)]
    for sweep_index in range(SWEEPS):
        micro_flux, tangent_local, linear_flux = evaluate(potential_now, sensitivity, mean_field, permeability, grain_axes, thresholds, hyst_axis, hyst_weight)
        weight_sum = tangent_local[0][0]
        for left_comp in range(3):
            for right_comp in range(3):
                if left_comp + right_comp > 0:
                    weight_sum = weight_sum + tangent_local[left_comp][right_comp]
        for component in range(3):
            weight_sum = weight_sum + neighbour(tangent_local[component][component], strides[component], False)
        diagonal_sum = diag_boost * weight_sum
        potential_now = potential_now + divergence(micro_flux) / diagonal_sum
        sensitivity = [sensitivity[column] + divergence([linear_flux[component][column] for component in range(3)]) / diagonal_sum for column in range(3)]
    micro_flux, tangent_local, linear_flux = evaluate(potential_now, sensitivity, mean_field, permeability, grain_axes, thresholds, hyst_axis, hyst_weight)
    mean_flux = [jnp.mean(micro_flux[component], axis=-1) for component in range(3)]
    mean_tangent = [jnp.mean(linear_flux[left_comp][column], axis=-1) for left_comp in range(3) for column in range(3)]
    return potential_now, mean_flux, mean_tangent


def reference(macro_field, rve_owner, potential, switch_words, permeability, coercivity, grain_axes, hyst_axis, hyst_low, hyst_high, hyst_weight, grad_weights, connectivity, node_order):
    blocks = N_SLAB * N_RVE
    target = rve_owner[:, 0].reshape(blocks, Q_DEV)
    owner_hits = (target[:, :, None] == jnp.arange(N_RVE, dtype=jnp.int32)[None, None, :]).astype(jnp.int32)
    earlier = (jnp.cumsum(owner_hits, axis=1) - owner_hits).astype(jnp.int32)
    rank_in = jnp.sum(earlier * owner_hits, axis=2).astype(jnp.int32)
    block_id = jnp.arange(blocks, dtype=jnp.int32)[:, None]
    row_index = ((((block_id // N_RVE) * N_RVE + target) * N_RVE + block_id % N_RVE) * CAP + rank_in).reshape(-1).astype(jnp.int32)
    portion = QUADS // N_SLAB
    word_rows = switch_words[row_index].reshape(N_SLAB, portion, VOX)
    perm_rows = permeability[row_index].reshape(N_SLAB, portion, VOX)
    coerc_rows = coercivity[row_index].reshape(N_SLAB, portion, VOX)
    grain_rows = grain_axes[:, row_index].reshape(3, N_SLAB, portion, VOX).transpose(1, 0, 2, 3)
    field_rows = macro_field.reshape(3, N_SLAB, portion).transpose(1, 0, 2)
    starts = potential.reshape(N_SLAB, portion, VOX)

    def solve_part(pieces):
        begin_phi, mean_in, words_in, perm_in, coerc_in, grain_in = pieces
        mean_field = [mean_in[component][:, None] for component in range(3)]
        grain_list = [grain_in[component] for component in range(3)]
        result, mean_flux, mean_tangent = micro_solve(begin_phi, mean_field, words_in, perm_in, coerc_in, grain_list, hyst_axis, hyst_low, hyst_high, hyst_weight)
        return result, jnp.stack(mean_flux), jnp.stack(mean_tangent)

    solved, fluxes, tangents = lax.map(solve_part, (starts, field_rows, word_rows, perm_rows, coerc_rows, grain_rows))
    potential_new = solved.reshape(QUADS, VOX)
    flux_point = fluxes.transpose(1, 0, 2).reshape(3, QUADS)
    tangent = tangents.transpose(1, 0, 2).reshape(3, 3, QUADS)
    nodal_terms = grad_weights[0] * flux_point[0][None, :] + grad_weights[1] * flux_point[1][None, :] + grad_weights[2] * flux_point[2][None, :]
    segment = (jnp.arange(QUADS, dtype=jnp.int32) // Q_DEV)[None, :] * NODES_LOC + connectivity
    local_sum = jax.ops.segment_sum(nodal_terms.reshape(-1), segment.reshape(-1).astype(jnp.int32), num_segments=NODES)
    orders = node_order.reshape(blocks, NODES_LOC)
    structured = jnp.take_along_axis(local_sum.reshape(blocks, NODES_LOC), orders, axis=1).reshape(N_SLAB, N_RVE, EX + 1, EY + 1, EZ + 1)
    from_left = jnp.pad(structured[:, :-1, EX], ((0, 0), (1, 0), (0, 0), (0, 0)))
    from_right = jnp.pad(structured[:, 1:, 0], ((0, 0), (0, 1), (0, 0), (0, 0)))
    summed = structured.at[:, :, 0].add(from_left).at[:, :, EX].add(from_right)
    from_below = jnp.pad(summed[:-1, :, :, EY], ((1, 0), (0, 0), (0, 0), (0, 0)))
    from_above = jnp.pad(summed[1:, :, :, 0], ((0, 1), (0, 0), (0, 0), (0, 0)))
    node_total = summed.at[:, :, :, 0].add(from_below).at[:, :, :, EY].add(from_above)
    residual = jnp.zeros((blocks, NODES_LOC), jnp.float32).at[jnp.arange(blocks, dtype=jnp.int32)[:, None], orders].set(node_total.reshape(blocks, NODES_LOC))
    return potential_new, tangent, residual.reshape(-1)
```

```python
import jax
import jax.numpy as jnp
from jax import lax
from jax.experimental import pallas as pl
from jax.experimental.pallas import tpu as pltpu
from jax.sharding import PartitionSpec as P

MESH = pl.DeviceIdType.MESH
f32 = jnp.float32
bf16 = jnp.bfloat16

GROUPS = 4
PEERS = 16
CAP = 4
SLOTS = PEERS * CAP
RVES = GROUPS * PEERS
SLABS = 8
PTS = 128
HALF = 256
NODES = 45

PERM = 0
GRAIN = 1
TH = 4
PG = 8
AIJ = 11
PHI = 17
PSI = 20
COER = 26
N_FIELDS = 27
PAIRS = ((0, 0), (0, 1), (0, 2), (1, 1), (1, 2), (2, 2))


def iota(shape, dim):
    return lax.broadcasted_iota(jnp.int32, shape, dim)


def dot(a, b):
    return lax.dot_general(a, b, (((1,), (0,)), ((), ())), precision=lax.Precision.HIGHEST,
                           preferred_element_type=f32)


def dot_t(a, b):
    return lax.dot_general(a, b, (((1,), (1,)), ((), ())), precision=lax.Precision.HIGHEST,
                           preferred_element_type=f32)


def pick(hot, data):
    hot = hot.astype(bf16)
    high = data.astype(bf16)
    low = (data - high.astype(f32)).astype(bf16)
    one = lax.dot_general(hot, high, (((1,), (0,)), ((), ())), preferred_element_type=f32)
    two = lax.dot_general(hot, low, (((1,), (0,)), ((), ())), preferred_element_type=f32)
    return one + two


def swap(v):
    return pltpu.roll(v, 64, v.ndim - 1)


def next_x(v):
    return jnp.concatenate([v[1:], swap(v[:1])], axis=0)


def prev_x(v):
    return jnp.concatenate([swap(v[3:]), v[:3]], axis=0)


def next_z(v):
    return pltpu.roll(v, 7, 1)


def prev_z(v):
    return pltpu.roll(v, 1, 1)


def recip(v):
    r = pl.reciprocal(v, approx=True)
    return r * (2.0 - v * r)


def sum_x(v):
    return (v[0] + v[1]) + (v[2] + v[3])


def to_rows(recv):
    n = recv.shape[-1]
    pairs = recv.reshape(8, 2, 8, n)
    even, odd = pairs[:, 0], pairs[:, 1]
    first = iota((8, 8, n), 1) < 4
    low = jnp.where(first, even, pltpu.roll(odd, 4, 1))
    high = jnp.where(first, pltpu.roll(even, 4, 1), odd)
    return jnp.concatenate([low.reshape(64, n), high.reshape(64, n)], axis=0)


def kernel(
    owner_ref, macro_ref, pot_ref, words_hbm, perm_hbm, coer_hbm, grain_hbm,
    axis_ref, low_ref, high_ref, weight_ref, gw_ref, conn_ref, order_ref,
    pot_out, tan_out, res_out,
    nat_words, nat_perm, nat_coer, nat_grain, words_t, fields,
    send_phi, send_mac, recv_phi, recv_mac, ret_phi, ret_val, back_phi, back_val,
    acc_ref, halo_src, halo_dst,
    load_sem, out_phi_send, out_phi_recv, out_mac_send, out_mac_recv,
    ret_phi_send, ret_phi_recv, ret_val_send, ret_val_recv, halo_send, halo_recv,
):
    me = lax.axis_index("rve")
    slab = lax.axis_index("slab")
    my_x = lax.div(me, PEERS)
    my_low = lax.rem(me, PEERS)
    right, left = lax.rem(me + 1, RVES), lax.rem(me + RVES - 1, RVES)
    above, below = lax.rem(slab + 1, SLABS), lax.rem(slab + SLABS - 1, SLABS)

    barrier = pltpu.get_barrier_semaphore()

    def greet(i, carry):
        peer = lax.rem(me + i, RVES)
        pl.semaphore_signal(barrier, inc=1, device_id=(slab, peer), device_id_type=MESH)
        return carry

    lax.fori_loop(1, RVES, greet, 0)
    for s in (above, below):
        for r in (left, me, right):
            pl.semaphore_signal(barrier, inc=1, device_id=(s, r), device_id_type=MESH)

    def loads(t):
        rows = pl.ds(lax.rem(my_x - t + GROUPS, GROUPS) * SLOTS, SLOTS)
        return (
            pltpu.make_async_copy(words_hbm.at[rows], nat_words.at[t], load_sem.at[0, t]),
            pltpu.make_async_copy(perm_hbm.at[rows], nat_perm.at[t], load_sem.at[1, t]),
            pltpu.make_async_copy(coer_hbm.at[rows], nat_coer.at[t], load_sem.at[2, t]),
            pltpu.make_async_copy(grain_hbm.at[:, rows], nat_grain.at[t], load_sem.at[3, t]),
        )

    for t in range(GROUPS):
        for copy in loads(t):
            copy.start()

    target_row = owner_ref[...]
    target_rows = jnp.broadcast_to(target_row.astype(f32), (PTS, PTS))
    target_cols = target_rows.T
    same = target_rows == target_cols
    q_row, q_col = iota((PTS, PTS), 1), iota((PTS, PTS), 0)
    rank_row = jnp.sum(jnp.where(same & (q_col < q_row), 1.0, 0.0), axis=0, keepdims=True).astype(jnp.int32)
    rank_col = jnp.sum(jnp.where(same & (q_row < q_col), 1.0, 0.0), axis=1, keepdims=True).astype(jnp.int32)
    target_col = target_cols[:, :1].astype(jnp.int32)
    place_row = target_row * 8 + rank_row
    place_col = target_col * 8 + rank_col

    slot_rows = iota((RVES * 8, PTS), 0)
    hot = jnp.concatenate([(slot_rows == place_row).astype(f32), (slot_rows == place_row + 4).astype(f32)], axis=1)
    halves = jnp.concatenate([pot_ref[:, :HALF], pot_ref[:, HALF:]], axis=0)
    send_phi[...] = pick(hot, halves).reshape(RVES, 8, HALF)

    n_rows = iota((PTS, PTS), 0)
    comp = n_rows // CAP
    spread = jnp.where(comp == 0, macro_ref[0:1], jnp.where(comp == 1, macro_ref[1:2], macro_ref[2:3]))
    spread = jnp.where((comp < 3) & (n_rows % CAP == rank_row), spread, 0.0)
    owner_hot = (iota((RVES, PTS), 0) == target_row).astype(f32)
    send_mac[...] = dot_t(owner_hot, spread).reshape(RVES, 1, PTS)

    pl.semaphore_wait(barrier, RVES - 1 + 6)

    def send(t):
        peer_x = lax.rem(my_x + t, GROUPS)

        def one(i, carry):
            peer = peer_x * PEERS + lax.rem(my_low + i, PEERS)

            @pl.when(peer != me)
            def _():
                pltpu.make_async_remote_copy(
                    src_ref=send_phi.at[peer], dst_ref=recv_phi.at[t, my_low],
                    send_sem=out_phi_send.at[t], recv_sem=out_phi_recv.at[t],
                    device_id=(slab, peer), device_id_type=MESH).start()
                pltpu.make_async_remote_copy(
                    src_ref=send_mac.at[peer], dst_ref=recv_mac.at[t, my_low],
                    send_sem=out_mac_send.at[t], recv_sem=out_mac_recv.at[t],
                    device_id=(slab, peer), device_id_type=MESH).start()

            @pl.when(peer == me)
            def _():
                pltpu.make_async_copy(send_phi.at[peer], recv_phi.at[t, my_low], out_phi_recv.at[t]).start()
                pltpu.make_async_copy(send_mac.at[peer], recv_mac.at[t, my_low], out_mac_recv.at[t]).start()

            return carry

        lax.fori_loop(0, PEERS, one, 0)

    for t in range(GROUPS):
        send(t)

    lane_peer = iota((PTS, PEERS), 0) // CAP % PEERS
    peer_t = (lane_peer == iota((PTS, PEERS), 1)).astype(f32)
    peer_m = (iota((PEERS, PTS), 1) // CAP % PEERS == iota((PEERS, PTS), 0)).astype(f32)
    mask_mac = iota((PTS, PTS), 0) % CAP == iota((PTS, PTS), 1) % CAP
    comp_m = (iota((8, PTS), 1) // CAP == iota((8, PTS), 0)).astype(f32)
    val_n = iota((PTS, 96), 0) % 32
    val_k = iota((PTS, 96), 1) // 8
    val_hot = jnp.where(
        jnp.where(val_k < 3, val_k, (val_k // 3) * 8 + val_k % 3) == val_n, 1.0 / 512.0, 0.0)
    mask_val = iota((PTS, PTS), 0) // 32 == iota((PTS, PTS), 1) % CAP

    axis2 = [[2.0 * axis_ref[c, k] for k in range(4)] for c in range(3)]
    mag_w = [[weight_ref[k] * axis_ref[c, k] for k in range(4)] for c in range(3)]
    pair_w = [[2.0 * weight_ref[k] * axis_ref[a, k] * axis_ref[b, k] for k in range(4)] for a, b in PAIRS]
    low2 = [2.0 * low_ref[k] for k in range(4)]
    high2 = [2.0 * high_ref[k] for k in range(4)]

    def evaluate(y, version, mean):
        now = fields[PHI + version, :, y]
        y_next = fields[PHI + version, :, lax.rem(y + 1, 8)]
        h = [mean[0] + (next_x(now) - now), mean[1] + (y_next - now), mean[2] + (next_z(now) - now)]
        g = [fields[GRAIN + c, :, y] * h[c] for c in range(3)]
        s = []
        for k in range(4):
            arg = axis2[0][k] * g[0] + axis2[1][k] * g[1] + axis2[2][k] * g[2] - fields[TH + k, :, y]
            s.append(jnp.tanh(arg))
        slope = [1.0 - v * v for v in s]
        perm = fields[PERM, :, y]
        flux = []
        for c in range(3):
            mag = mag_w[c][0] * s[0] + mag_w[c][1] * s[1] + mag_w[c][2] * s[2] + mag_w[c][3] * s[3]
            flux.append(perm * h[c] + fields[PG + c, :, y] * mag)
        stiff = {}
        for i, pair in enumerate(PAIRS):
            w = pair_w[i]
            total = w[0] * slope[0] + w[1] * slope[1] + w[2] * slope[2] + w[3] * slope[3]
            v = fields[AIJ + i, :, y] * total
            if pair[0] == pair[1]:
                v = v + perm
            stiff[pair] = v
            stiff[pair[::-1]] = v
        return now, flux, stiff

    def sweep_body(y, first, mean, carry):
        now, flux, stiff = evaluate(y, 0 if first else 1, mean)
        if first:
            lin = stiff
        else:
            lin = {}
            psi = [fields[PSI + d, :, y] for d in range(3)]
            psi_y = [fields[PSI + d, :, lax.rem(y + 1, 8)] for d in range(3)]
            for d in range(3):
                grad = [next_x(psi[d]) - psi[d], psi_y[d] - psi[d], next_z(psi[d]) - psi[d]]
                grad[d] = grad[d] + 1.0
                for c in range(3):
                    lin[c, d] = stiff[c, 0] * grad[0] + stiff[c, 1] * grad[1] + stiff[c, 2] * grad[2]
        nxt = (flux[1], stiff[1, 1], lin[1, 0], lin[1, 1], lin[1, 2])
        cross = stiff[0, 1] + stiff[0, 2] + stiff[1, 2]
        weight = (stiff[0, 0] + stiff[1, 1] + stiff[2, 2] + (cross + cross)
                  + prev_x(stiff[0, 0]) + prev_z(stiff[2, 2]))
        force = (flux[0] - prev_x(flux[0])) + flux[1] + (flux[2] - prev_z(flux[2]))
        forces = [(lin[0, d] - prev_x(lin[0, d])) + lin[1, d] + (lin[2, d] - prev_z(lin[2, d])) for d in range(3)]
        if carry is not None:
            force, weight, forces = close(force, weight, forces, carry)
        return nxt, (force, weight, forces)

    def close(force, weight, forces, carry):
        return force - carry[0], weight + carry[1], [forces[d] - carry[2 + d] for d in range(3)]

    def apply(y, first, sums):
        force, weight, forces = sums
        inv = recip(1.5 * weight)
        old, new = (0, 1) if first else (1, 2)
        fields[PHI + new, :, y] = fields[PHI + old, :, y] + force * inv
        for d in range(3):
            step = forces[d] * inv
            if not first:
                step = fields[PSI + d, :, y] + step
            fields[PSI + (0 if first else 3) + d, :, y] = step

    def sweep(first, mean):
        carry, (force, weight, forces) = sweep_body(0, first, mean, None)

        def step(y, carry):
            nxt, sums = sweep_body(y, first, mean, carry)
            apply(y, first, sums)
            return nxt

        carry = lax.fori_loop(1, 8, step, carry)
        apply(0, first, close(force, weight, forces, carry))

    def last(mean):
        def step(y, carry):
            prev, acc = carry
            now, flux, stiff = evaluate(y, 2, mean)
            psi = [fields[PSI + 3 + d, :, y] for d in range(3)]
            acc = list(acc)
            for c in range(3):
                acc[c] = acc[c] + sum_x(flux[c])
            for i, pair in enumerate(PAIRS):
                acc[3 + i] = acc[3 + i] + sum_x(stiff[pair])
            for c in range(3):
                div = ((stiff[0, c] - prev_x(stiff[0, c])) + (stiff[1, c] - prev[c])
                       + (stiff[2, c] - prev_z(stiff[2, c])))
                for d in range(3):
                    acc[9 + 3 * c + d] = acc[9 + 3 * c + d] + sum_x(div * psi[d])
            return (stiff[0, 1], stiff[1, 1], stiff[1, 2]), tuple(acc)

        zero = jnp.zeros((4, 8, PTS), f32)
        flat = jnp.zeros((8, PTS), f32)
        prev, acc = lax.fori_loop(0, 8, step, ((zero,) * 3, (flat,) * 18))
        psi = [fields[PSI + 3 + d, :, 0] for d in range(3)]
        for c in range(3):
            acc_ref[8 * c:8 * c + 8] = acc[c]
            for d in range(3):
                pair = PAIRS.index((min(c, d), max(c, d)))
                k = 3 + 3 * c + d
                acc_ref[8 * k:8 * k + 8] = acc[3 + pair] - acc[9 + 3 * c + d] + sum_x(prev[c] * psi[d])

    def turn(nat, h):
        a = nat[:, h * PTS:(h + 1) * PTS]
        b = nat[:, HALF + h * PTS:HALF + (h + 1) * PTS]
        return jnp.concatenate([a, b], axis=0).T.reshape(2, 8, 8, PTS)

    def group(t, carry):
        for copy in loads(t):
            copy.wait()
        for h in range(2):
            xs = slice(2 * h, 2 * h + 2)
            words_t[xs] = turn(nat_words[t], h)
            fields[COER, xs] = turn(nat_coer[t], h)
            fields[PERM, xs] = turn(nat_perm[t], h)
            for c in range(3):
                fields[GRAIN + c, xs] = turn(nat_grain[t, c], h)

        def prepare(y, carry):
            words = words_t[:, y]
            coer = fields[COER, :, y]
            for k in range(4):
                up = jnp.bitwise_and(words, 1 << k) != 0
                fields[TH + k, :, y] = coer * jnp.where(up, low2[k], high2[k])
            perm = fields[PERM, :, y]
            grain = [fields[GRAIN + c, :, y] for c in range(3)]
            pg = [perm * grain[c] for c in range(3)]
            for c in range(3):
                fields[PG + c, :, y] = pg[c]
            for i, (a, b) in enumerate(PAIRS):
                fields[AIJ + i, :, y] = pg[a] * grain[b]
            return carry

        lax.fori_loop(0, 8, prepare, 0)

        pltpu.make_async_copy(recv_phi.at[t], recv_phi.at[t], out_phi_recv.at[t]).wait()
        pltpu.make_async_copy(recv_mac.at[t], recv_mac.at[t], out_mac_recv.at[t]).wait()
        rows = to_rows(recv_phi[t])
        for h in range(2):
            fields[PHI, 2 * h:2 * h + 2] = rows[:, h * PTS:(h + 1) * PTS].T.reshape(2, 8, 8, PTS)
        mac = dot(peer_t, recv_mac[t, :, 0, :])
        mac = dot_t(comp_m, jnp.where(mask_mac, mac, 0.0))
        mean = [jnp.broadcast_to(mac[c:c + 1], (8, PTS))[None] for c in range(3)]

        sweep(True, mean)
        sweep(False, mean)

        first = iota((8, 8, PTS), 1) < 4
        for h in range(2):
            block = fields[PHI + 2, 2 * h:2 * h + 2].reshape(PTS, PTS).T.reshape(2, 8, 8, PTS)
            low, high = block[0], block[1]
            cols = slice(h * PTS, (h + 1) * PTS)
            ret_phi[t, :, 0, :, cols] = jnp.where(first, low, pltpu.roll(high, 4, 1))
            ret_phi[t, :, 1, :, cols] = jnp.where(first, pltpu.roll(low, 4, 1), high)

        src_x = lax.rem(my_x - t + GROUPS, GROUPS)

        def give(src, dst, send_sem, recv_sem):
            def one(i, carry):
                low = lax.rem(my_low + i, PEERS)
                peer = src_x * PEERS + low
                piece = src(low)

                @pl.when(peer != me)
                def _():
                    pltpu.make_async_remote_copy(
                        src_ref=piece, dst_ref=dst.at[me], send_sem=send_sem.at[t], recv_sem=recv_sem.at[t],
                        device_id=(slab, peer), device_id_type=MESH).start()

                @pl.when(peer == me)
                def _():
                    pltpu.make_async_copy(piece, dst.at[me], recv_sem.at[t]).start()

                return carry

            lax.fori_loop(0, PEERS, one, 0)

        give(lambda low: ret_phi.at[t, lax.div(low, 2), lax.rem(low, 2)], back_phi, ret_phi_send, ret_phi_recv)
        last(mean)
        val = jnp.where(mask_val, dot(val_hot, acc_ref[...]), 0.0)
        ret_val[t] = dot_t(peer_m, val).reshape(PEERS, 1, PTS)
        give(lambda low: ret_val.at[t, low], back_val, ret_val_send, ret_val_recv)
        return carry

    lax.fori_loop(0, GROUPS, group, 0)

    for t in range(GROUPS):
        mine = back_val.at[pl.ds(lax.rem(my_x + t, GROUPS) * PEERS, PEERS)]
        pltpu.make_async_copy(mine, mine, ret_val_recv.at[t]).wait()
    owner_col = (iota((PTS, RVES), 1) == target_col).astype(f32)
    vals = dot(owner_col, back_val[:, 0, :])
    vals = jnp.where(iota((PTS, PTS), 1) // 32 == rank_col, vals, 0.0)
    fold = (iota((32, PTS), 1) % 32 == iota((32, PTS), 0)).astype(f32)
    point = dot_t(fold, vals)
    for c in range(3):
        tan_out[c] = point[8 * c + 8:8 * c + 11]

    nodal = gw_ref[0] * point[0:1] + gw_ref[1] * point[1:2] + gw_ref[2] * point[2:3]
    conn = conn_ref[...]
    node_rows = iota((PTS, PTS), 0)
    spread = jnp.zeros((PTS, PTS), f32)
    for a in range(8):
        spread = spread + jnp.where(conn[a:a + 1] == node_rows, nodal[a:a + 1], 0.0)
    local = dot_t(jnp.ones((8, PTS), f32), spread)
    order = order_ref[...]
    order_hot = (iota((PTS, PTS), 0) == order).astype(f32)
    grid = dot(local, order_hot)[0:1]
    halo_src[...] = grid
    turns = [(ds, dr) for ds in (-1, 0, 1) for dr in (-1, 0, 1) if (ds, dr) != (0, 0)]
    copies = []
    for i, (ds, dr) in enumerate(turns):
        to_slab = (below, slab, above)[ds + 1]
        to_rve = (left, me, right)[dr + 1]
        copies.append(pltpu.make_async_remote_copy(
            src_ref=halo_src, dst_ref=halo_dst.at[i], send_sem=halo_send.at[i], recv_sem=halo_recv.at[i],
            device_id=(to_slab, to_rve), device_id_type=MESH))
        copies[i].start()

    for t in range(GROUPS):
        mine = back_phi.at[pl.ds(lax.rem(my_x + t, GROUPS) * PEERS, PEERS)]
        pltpu.make_async_copy(mine, mine, ret_phi_recv.at[t]).wait()
    slot_cols = iota((PTS, RVES * 8), 1)
    hot = jnp.concatenate([(slot_cols == place_col).astype(f32), (slot_cols == place_col + 4).astype(f32)], axis=0)
    found = pick(hot, back_phi[...].reshape(RVES * 8, HALF))
    pot_out[:, :HALF] = found[:PTS]
    pot_out[:, HALF:] = found[PTS:]

    lane = iota((1, PTS), 1)
    at_i, at_j = lane // 15, lane // 5 % 3
    total = grid
    for i, (ds, dr) in enumerate(turns):
        copies[i].wait_recv()
        ok = lane < NODES
        if dr != 0:
            ok = ok & (at_i == (0 if dr > 0 else 2)) & ((me > 0) if dr > 0 else (me < RVES - 1))
        if ds != 0:
            ok = ok & (at_j == (0 if ds > 0 else 2)) & ((slab > 0) if ds > 0 else (slab < SLABS - 1))
        shift = (-30 * dr - 10 * ds) % PTS
        moved = pltpu.roll(jnp.broadcast_to(halo_dst[i], (8, PTS)), shift, 1)[0:1]
        total = total + jnp.where(ok, moved, 0.0)
    total = jnp.where(lane < NODES, total, 0.0)
    back = dot_t(jnp.broadcast_to(total, (8, PTS)), order_hot)
    res_out[...] = back[0:1, :NODES]

    for copy in copies:
        copy.wait_send()
    for t in range(GROUPS):
        n = PEERS - 1 if t == 0 else PEERS
        pltpu.make_async_copy(send_phi.at[pl.ds(0, n)], send_phi.at[pl.ds(0, n)], out_phi_send.at[t]).wait()
        pltpu.make_async_copy(send_mac.at[pl.ds(0, n)], send_mac.at[pl.ds(0, n)], out_mac_send.at[t]).wait()
        pltpu.make_async_copy(send_phi.at[pl.ds(0, n)], send_phi.at[pl.ds(0, n)], ret_phi_send.at[t]).wait()
        pltpu.make_async_copy(send_mac.at[pl.ds(0, n)], send_mac.at[pl.ds(0, n)], ret_val_send.at[t]).wait()


def on_device(
    macro_field, rve_owner, potential, switch_words, permeability, coercivity, grain_axes,
    hyst_axis, hyst_low, hyst_high, hyst_weight, grad_weights, connectivity, node_order,
):
    vmem = pl.BlockSpec(memory_space=pltpu.VMEM)
    smem = pl.BlockSpec(memory_space=pltpu.SMEM)
    hbm = pl.BlockSpec(memory_space=pl.ANY)
    order = jnp.pad(node_order, (0, PTS - NODES), constant_values=-1).reshape(1, PTS)
    pot, tan, res = pl.pallas_call(
        kernel,
        out_shape=(
            jax.ShapeDtypeStruct((PTS, 2 * HALF), f32),
            jax.ShapeDtypeStruct((3, 3, PTS), f32),
            jax.ShapeDtypeStruct((1, NODES), f32),
        ),
        in_specs=[vmem, vmem, vmem, hbm, hbm, hbm, hbm, smem, smem, smem, smem, vmem, vmem, vmem],
        out_specs=(vmem, vmem, vmem),
        scratch_shapes=[
            pltpu.VMEM((GROUPS, SLOTS, 2 * HALF), jnp.int32),
            pltpu.VMEM((GROUPS, SLOTS, 2 * HALF), f32),
            pltpu.VMEM((GROUPS, SLOTS, 2 * HALF), f32),
            pltpu.VMEM((GROUPS, 3, SLOTS, 2 * HALF), f32),
            pltpu.VMEM((4, 8, 8, PTS), jnp.int32),
            pltpu.VMEM((N_FIELDS, 4, 8, 8, PTS), f32),
            pltpu.VMEM((RVES, 8, HALF), f32),
            pltpu.VMEM((RVES, 1, PTS), f32),
            pltpu.VMEM((GROUPS, PEERS, 8, HALF), f32),
            pltpu.VMEM((GROUPS, PEERS, 1, PTS), f32),
            pltpu.VMEM((GROUPS, PEERS // 2, 2, 8, HALF), f32),
            pltpu.VMEM((GROUPS, PEERS, 1, PTS), f32),
            pltpu.VMEM((RVES, 8, HALF), f32),
            pltpu.VMEM((RVES, 1, PTS), f32),
            pltpu.VMEM((96, PTS), f32),
            pltpu.VMEM((1, PTS), f32),
            pltpu.VMEM((8, 1, PTS), f32),
            pltpu.SemaphoreType.DMA((4, GROUPS)),
        ] + [pltpu.SemaphoreType.DMA((GROUPS,))] * 8 + [pltpu.SemaphoreType.DMA((8,))] * 2,
        compiler_params=pltpu.CompilerParams(
            collective_id=0, has_side_effects=True, vmem_limit_bytes=48 * 1024 * 1024),
    )(rve_owner.reshape(1, PTS), macro_field, potential, switch_words, permeability, coercivity, grain_axes,
      hyst_axis, hyst_low, hyst_high, hyst_weight, grad_weights, connectivity, order)
    return pot, tan, res.reshape(NODES)


def solution(mesh):
    return jax.shard_map(
        on_device,
        mesh=mesh,
        in_specs=(
            P(None, ("slab", "rve")),
            P(("slab", "rve"), None),
            P(("slab", "rve"), None),
            P(("slab", "rve"), None),
            P(("slab", "rve"), None),
            P(("slab", "rve"), None),
            P(None, ("slab", "rve"), None),
            P(),
            P(),
            P(),
            P(),
            P(None, None, ("slab", "rve")),
            P(None, ("slab", "rve")),
            P(("slab", "rve")),
        ),
        out_specs=(P(("slab", "rve"), None), P(None, None, ("slab", "rve")), P(("slab", "rve"))),
        check_vma=False,
    )
```

```python
import jax
import jax.numpy as jnp
from jax import lax
from jax.experimental import pallas as pl
from jax.experimental.pallas import tpu as pltpu
from jax.sharding import PartitionSpec as P

MESH = pl.DeviceIdType.MESH
f32 = jnp.float32
bf16 = jnp.bfloat16

GROUPS = 4
PEERS = 16
CAP = 4
SLOTS = PEERS * CAP
RVES = GROUPS * PEERS
SLABS = 8
PTS = 128
HALF = 256
NODES = 45
ROWS = 48
UNROLL = (7, 7, 8, 8)

PERM = 0
GRAIN = 1
TH = 4
PG = 8
AIJ = 11
PHI = 17
PSI = 20
COER = 26
N_FIELDS = 27
PAIRS = ((0, 0), (0, 1), (0, 2), (1, 1), (1, 2), (2, 2))


def iota(shape, dim):
    return lax.broadcasted_iota(jnp.int32, shape, dim)


def parts(data):
    high = data.astype(bf16)
    return high, (data - high.astype(f32)).astype(bf16)


def mm(a, b, dim):
    return lax.dot_general(a, b, (((1,), (dim,)), ((), ())), preferred_element_type=f32)


def dot(hot, data):
    high, low = parts(data)
    hot = hot.astype(bf16)
    return mm(hot, high, 0) + mm(hot, low, 0)


def dot_t(hot, data):
    high, low = parts(data)
    hot = hot.astype(bf16)
    return mm(hot, high, 1) + mm(hot, low, 1)


def swap(v):
    return pltpu.roll(v, 64, v.ndim - 1)


def next_x(v):
    return jnp.concatenate([v[1:], swap(v[:1])], axis=0)


def prev_x(v):
    return jnp.concatenate([swap(v[3:]), v[:3]], axis=0)


def next_z(v):
    return pltpu.roll(v, 7, 1)


def prev_z(v):
    return pltpu.roll(v, 1, 1)


def recip(v):
    r = pl.reciprocal(v, approx=True)
    return r * (2.0 - v * r)


def sum_x(v):
    return (v[0] + v[1]) + (v[2] + v[3])


def to_rows(recv):
    n = recv.shape[-1]
    pairs = recv.reshape(8, 2, 8, n)
    even, odd = pairs[:, 0], pairs[:, 1]
    first = iota((8, 8, n), 1) < 4
    low = jnp.where(first, even, pltpu.roll(odd, 4, 1))
    high = jnp.where(first, pltpu.roll(even, 4, 1), odd)
    return jnp.concatenate([low.reshape(64, n), high.reshape(64, n)], axis=0)


def kernel(
    owner_hbm, macro_hbm, pot_hbm, words_hbm, perm_hbm, coer_hbm, grain_hbm,
    axis_hbm, low_hbm, high_hbm, weight_hbm, gw_hbm, conn_hbm, order_hbm,
    pot_out, tan_out, res_out,
    owner_ref, macro_ref, pot_ref, axis_ref, low_ref, high_ref, weight_ref, gw_ref, conn_ref, order_ref, early_sem,
    nat_words, nat_perm, nat_coer, nat_grain, words_t, fields,
    send_phi, send_mac, recv_phi, recv_mac, ret_phi, ret_val, back_phi, back_val,
    acc_ref, halo_src, halo_dst,
    load_sem, out_phi_send, out_phi_recv, out_mac_send, out_mac_recv,
    ret_phi_send, ret_phi_recv, ret_val_send, ret_val_recv, halo_send, halo_recv,
):
    me = lax.axis_index("rve")
    slab = lax.axis_index("slab")
    my_x = lax.div(me, PEERS)
    my_low = lax.rem(me, PEERS)
    right, left = lax.rem(me + 1, RVES), lax.rem(me + RVES - 1, RVES)

    barrier = pltpu.get_barrier_semaphore()

    def greet(i, carry):
        peer = lax.rem(me + i, RVES)
        pl.semaphore_signal(barrier, inc=1, device_id=(slab, peer), device_id_type=MESH)
        return carry

    lax.fori_loop(1, RVES, greet, 0)

    def toward(ds, action):
        if ds == 0:
            action()
        else:
            pl.when((slab > 0) if ds < 0 else (slab < SLABS - 1))(action)

    for ds in (-1, 1):
        def hail(ds=ds):
            for r in (left, me, right):
                pl.semaphore_signal(barrier, inc=1, device_id=(slab + ds, r), device_id_type=MESH)

        toward(ds, hail)

    early = [
        pltpu.make_async_copy(src, dst, early_sem.at[i])
        for i, (src, dst) in enumerate((
            (owner_hbm, owner_ref), (pot_hbm, pot_ref), (macro_hbm, macro_ref), (axis_hbm, axis_ref),
            (low_hbm, low_ref), (high_hbm, high_ref), (weight_hbm, weight_ref), (gw_hbm, gw_ref),
            (conn_hbm, conn_ref), (order_hbm, order_ref)))
    ]
    for copy in early:
        copy.start()

    def loads(t):
        rows = pl.ds(lax.rem(my_x - t + GROUPS, GROUPS) * SLOTS, SLOTS)
        return (
            pltpu.make_async_copy(words_hbm.at[rows], nat_words.at[t], load_sem.at[0, t]),
            pltpu.make_async_copy(perm_hbm.at[rows], nat_perm.at[t], load_sem.at[1, t]),
            pltpu.make_async_copy(coer_hbm.at[rows], nat_coer.at[t], load_sem.at[2, t]),
            pltpu.make_async_copy(grain_hbm.at[:, rows], nat_grain.at[t], load_sem.at[3, t]),
        )

    for t in range(GROUPS):
        for copy in loads(t):
            copy.start()

    early[0].wait()
    target_row = owner_ref[...]
    target_rows = jnp.broadcast_to(target_row.astype(f32), (PTS, PTS))
    target_cols = target_rows.T
    same = target_rows == target_cols
    q_row, q_col = iota((PTS, PTS), 1), iota((PTS, PTS), 0)
    rank_row = jnp.sum(jnp.where(same & (q_col < q_row), 1.0, 0.0), axis=0, keepdims=True).astype(jnp.int32)
    rank_col = jnp.sum(jnp.where(same & (q_row < q_col), 1.0, 0.0), axis=1, keepdims=True).astype(jnp.int32)
    target_col = target_cols[:, :1].astype(jnp.int32)
    place_row = target_row * 8 + rank_row
    place_col = target_col * 8 + rank_col

    for copy in early[1:]:
        copy.wait()
    slot_rows = iota((RVES * 8, PTS), 0)
    hot = jnp.concatenate([(slot_rows == place_row).astype(f32), (slot_rows == place_row + 4).astype(f32)], axis=1)
    halves = jnp.concatenate([pot_ref[:, :HALF], pot_ref[:, HALF:]], axis=0)
    send_phi[...] = dot(hot, halves).reshape(RVES, 8, HALF)

    n_rows = iota((PTS, PTS), 0)
    comp = n_rows // CAP
    spread = jnp.where(comp == 0, macro_ref[0:1], jnp.where(comp == 1, macro_ref[1:2], macro_ref[2:3]))
    spread = jnp.where((comp < 3) & (n_rows % CAP == rank_row), spread, 0.0)
    owner_hot = (iota((RVES, PTS), 0) == target_row).astype(f32)
    send_mac[...] = dot_t(owner_hot, spread).reshape(RVES, 1, PTS)

    sides = lax.div(slab + SLABS - 1, SLABS) + lax.div(2 * SLABS - 2 - slab, SLABS)
    pl.semaphore_wait(barrier, RVES - 1 + 3 * sides)

    def partner(i):
        k = lax.div(i, 2)
        step = lax.div(k + 1, 2) * (2 * lax.rem(k, 2) - 1)
        return lax.rem(my_low + 2 * step + PEERS + lax.rem(i, 2) * (1 - 2 * lax.rem(my_low, 2)), PEERS)

    def send(t):
        peer_x = lax.rem(my_x + t, GROUPS)

        def one(i, carry):
            peer = peer_x * PEERS + partner(i)

            @pl.when(peer != me)
            def _():
                pltpu.make_async_remote_copy(
                    src_ref=send_phi.at[peer], dst_ref=recv_phi.at[t, my_low],
                    send_sem=out_phi_send.at[t], recv_sem=out_phi_recv.at[t],
                    device_id=(slab, peer), device_id_type=MESH).start()
                pltpu.make_async_remote_copy(
                    src_ref=send_mac.at[peer], dst_ref=recv_mac.at[t, my_low],
                    send_sem=out_mac_send.at[t], recv_sem=out_mac_recv.at[t],
                    device_id=(slab, peer), device_id_type=MESH).start()

            @pl.when(peer == me)
            def _():
                pltpu.make_async_copy(send_phi.at[peer], recv_phi.at[t, my_low], out_phi_recv.at[t]).start()
                pltpu.make_async_copy(send_mac.at[peer], recv_mac.at[t, my_low], out_mac_recv.at[t]).start()

            return carry

        lax.fori_loop(0, PEERS, one, 0)

    for t in range(GROUPS):
        send(t)

    order_row = jnp.sum(jnp.where(iota((PTS, NODES), 0) == iota((PTS, NODES), 1), order_ref[...].astype(f32), 0.0),
                        axis=1, keepdims=True)
    order_cols = jnp.where(iota((PTS, PTS), 0) < NODES, jnp.broadcast_to(order_row, (PTS, PTS)), -1.0)
    order_row = order_cols.T[:1].astype(jnp.int32)
    order_col = order_cols[:ROWS].astype(jnp.int32)

    lane_peer = iota((PTS, PEERS), 0) // CAP % PEERS
    peer_t = (lane_peer == iota((PTS, PEERS), 1)).astype(f32)
    peer_m = (iota((PEERS, PTS), 1) // CAP % PEERS == iota((PEERS, PTS), 0)).astype(f32)
    mask_mac = iota((PTS, PTS), 0) % CAP == iota((PTS, PTS), 1) % CAP
    comp_m = (iota((8, PTS), 1) // CAP == iota((8, PTS), 0)).astype(f32)
    val_n = iota((PTS, 96), 0) % 32
    val_k = iota((PTS, 96), 1) // 8
    val_hot = jnp.where(
        jnp.where(val_k < 3, val_k, (val_k // 3) * 8 + val_k % 3) == val_n, 1.0 / 512.0, 0.0)
    mask_val = iota((PTS, PTS), 0) // 32 == iota((PTS, PTS), 1) % CAP

    axis2 = [[2.0 * axis_ref[c, k] for k in range(4)] for c in range(3)]
    mag_w = [[weight_ref[k] * axis_ref[c, k] for k in range(4)] for c in range(3)]
    pair_w = [[2.0 * weight_ref[k] * axis_ref[a, k] * axis_ref[b, k] for k in range(4)] for a, b in PAIRS]
    low2 = [2.0 * low_ref[k] for k in range(4)]
    high2 = [2.0 * high_ref[k] for k in range(4)]

    def evaluate(y, version, mean):
        now = fields[PHI + version, :, y]
        y_next = fields[PHI + version, :, lax.rem(y + 1, 8)]
        h = [mean[0] + (next_x(now) - now), mean[1] + (y_next - now), mean[2] + (next_z(now) - now)]
        g = [fields[GRAIN + c, :, y] * h[c] for c in range(3)]
        s = []
        for k in range(4):
            arg = axis2[0][k] * g[0] + axis2[1][k] * g[1] + axis2[2][k] * g[2] - fields[TH + k, :, y]
            s.append(jnp.tanh(arg))
        slope = [1.0 - v * v for v in s]
        perm = fields[PERM, :, y]
        flux = []
        for c in range(3):
            mag = mag_w[c][0] * s[0] + mag_w[c][1] * s[1] + mag_w[c][2] * s[2] + mag_w[c][3] * s[3]
            flux.append(perm * h[c] + fields[PG + c, :, y] * mag)
        stiff = {}
        for i, pair in enumerate(PAIRS):
            w = pair_w[i]
            total = w[0] * slope[0] + w[1] * slope[1] + w[2] * slope[2] + w[3] * slope[3]
            v = fields[AIJ + i, :, y] * total
            if pair[0] == pair[1]:
                v = v + perm
            stiff[pair] = v
            stiff[pair[::-1]] = v
        return now, flux, stiff

    def sweep_body(y, first, mean, carry):
        now, flux, stiff = evaluate(y, 0 if first else 1, mean)
        if first:
            lin = stiff
        else:
            lin = {}
            psi = [fields[PSI + d, :, y] for d in range(3)]
            psi_y = [fields[PSI + d, :, lax.rem(y + 1, 8)] for d in range(3)]
            for d in range(3):
                grad = [next_x(psi[d]) - psi[d], psi_y[d] - psi[d], next_z(psi[d]) - psi[d]]
                grad[d] = grad[d] + 1.0
                for c in range(3):
                    lin[c, d] = stiff[c, 0] * grad[0] + stiff[c, 1] * grad[1] + stiff[c, 2] * grad[2]
        nxt = (flux[1], stiff[1, 1], lin[1, 0], lin[1, 1], lin[1, 2])
        cross = stiff[0, 1] + stiff[0, 2] + stiff[1, 2]
        weight = (stiff[0, 0] + stiff[1, 1] + stiff[2, 2] + (cross + cross)
                  + prev_x(stiff[0, 0]) + prev_z(stiff[2, 2]))
        force = (flux[0] - prev_x(flux[0])) + flux[1] + (flux[2] - prev_z(flux[2]))
        forces = [(lin[0, d] - prev_x(lin[0, d])) + lin[1, d] + (lin[2, d] - prev_z(lin[2, d])) for d in range(3)]
        if carry is not None:
            force, weight, forces = close(force, weight, forces, carry)
        return nxt, (force, weight, forces)

    def close(force, weight, forces, carry):
        return force - carry[0], weight + carry[1], [forces[d] - carry[2 + d] for d in range(3)]

    def apply(y, first, sums):
        force, weight, forces = sums
        inv = recip(1.5 * weight)
        old, new = (0, 1) if first else (1, 2)
        fields[PHI + new, :, y] = fields[PHI + old, :, y] + force * inv
        for d in range(3):
            step = forces[d] * inv
            if not first:
                step = fields[PSI + d, :, y] + step
            fields[PSI + (0 if first else 3) + d, :, y] = step

    def sweep(first, mean):
        carry, (force, weight, forces) = sweep_body(0, first, mean, None)

        def step(y, carry):
            nxt, sums = sweep_body(y, first, mean, carry)
            apply(y, first, sums)
            return nxt

        carry = lax.fori_loop(1, 8, step, carry, unroll=UNROLL[0 if first else 1])
        apply(0, first, close(force, weight, forces, carry))

    def last(mean):
        def step(y, carry):
            prev, acc = carry
            now, flux, stiff = evaluate(y, 2, mean)
            psi = [fields[PSI + 3 + d, :, y] for d in range(3)]
            acc = list(acc)
            for c in range(3):
                acc[c] = acc[c] + sum_x(flux[c])
            for i, pair in enumerate(PAIRS):
                acc[3 + i] = acc[3 + i] + sum_x(stiff[pair])
            for c in range(3):
                div = ((stiff[0, c] - prev_x(stiff[0, c])) + (stiff[1, c] - prev[c])
                       + (stiff[2, c] - prev_z(stiff[2, c])))
                for d in range(3):
                    acc[9 + 3 * c + d] = acc[9 + 3 * c + d] + sum_x(div * psi[d])
            return (stiff[0, 1], stiff[1, 1], stiff[1, 2]), tuple(acc)

        zero = jnp.zeros((4, 8, PTS), f32)
        flat = jnp.zeros((8, PTS), f32)
        prev, acc = lax.fori_loop(0, 8, step, ((zero,) * 3, (flat,) * 18), unroll=UNROLL[2])
        psi = [fields[PSI + 3 + d, :, 0] for d in range(3)]
        for c in range(3):
            acc_ref[8 * c:8 * c + 8] = acc[c]
            for d in range(3):
                pair = PAIRS.index((min(c, d), max(c, d)))
                k = 3 + 3 * c + d
                acc_ref[8 * k:8 * k + 8] = acc[3 + pair] - acc[9 + 3 * c + d] + sum_x(prev[c] * psi[d])

    def turn(nat, h):
        a = nat[:, h * PTS:(h + 1) * PTS]
        b = nat[:, HALF + h * PTS:HALF + (h + 1) * PTS]
        return jnp.concatenate([a, b], axis=0).T.reshape(2, 8, 8, PTS)

    def group(t, carry):
        for copy in loads(t):
            copy.wait()
        for h in range(2):
            xs = slice(2 * h, 2 * h + 2)
            words_t[xs] = turn(nat_words[t], h)
            fields[COER, xs] = turn(nat_coer[t], h)
            fields[PERM, xs] = turn(nat_perm[t], h)
            for c in range(3):
                fields[GRAIN + c, xs] = turn(nat_grain[t, c], h)

        def prepare(y, carry):
            words = words_t[:, y]
            coer = fields[COER, :, y]
            for k in range(4):
                up = jnp.bitwise_and(words, 1 << k) != 0
                fields[TH + k, :, y] = coer * jnp.where(up, low2[k], high2[k])
            perm = fields[PERM, :, y]
            grain = [fields[GRAIN + c, :, y] for c in range(3)]
            pg = [perm * grain[c] for c in range(3)]
            for c in range(3):
                fields[PG + c, :, y] = pg[c]
            for i, (a, b) in enumerate(PAIRS):
                fields[AIJ + i, :, y] = pg[a] * grain[b]
            return carry

        lax.fori_loop(0, 8, prepare, 0, unroll=UNROLL[3])

        pltpu.make_async_copy(recv_phi.at[t], recv_phi.at[t], out_phi_recv.at[t]).wait()
        pltpu.make_async_copy(recv_mac.at[t], recv_mac.at[t], out_mac_recv.at[t]).wait()
        rows = to_rows(recv_phi[t])
        for h in range(2):
            fields[PHI, 2 * h:2 * h + 2] = rows[:, h * PTS:(h + 1) * PTS].T.reshape(2, 8, 8, PTS)
        mac = dot(peer_t, recv_mac[t, :, 0, :])
        mac = dot_t(comp_m, jnp.where(mask_mac, mac, 0.0))
        mean = [jnp.broadcast_to(mac[c:c + 1], (8, PTS))[None] for c in range(3)]

        sweep(True, mean)
        sweep(False, mean)

        first = iota((8, 8, PTS), 1) < 4
        for h in range(2):
            block = fields[PHI + 2, 2 * h:2 * h + 2].reshape(PTS, PTS).T.reshape(2, 8, 8, PTS)
            low, high = block[0], block[1]
            cols = slice(h * PTS, (h + 1) * PTS)
            ret_phi[t, :, 0, :, cols] = jnp.where(first, low, pltpu.roll(high, 4, 1))
            ret_phi[t, :, 1, :, cols] = jnp.where(first, pltpu.roll(low, 4, 1), high)

        src_x = lax.rem(my_x - t + GROUPS, GROUPS)

        def give(src, dst, send_sem, recv_sem):
            def one(i, carry):
                low = partner(i)
                peer = src_x * PEERS + low
                piece = src(low)

                @pl.when(peer != me)
                def _():
                    pltpu.make_async_remote_copy(
                        src_ref=piece, dst_ref=dst.at[me], send_sem=send_sem.at[t], recv_sem=recv_sem.at[t],
                        device_id=(slab, peer), device_id_type=MESH).start()

                @pl.when(peer == me)
                def _():
                    pltpu.make_async_copy(piece, dst.at[me], recv_sem.at[t]).start()

                return carry

            lax.fori_loop(0, PEERS, one, 0)

        def give_phi():
            give(lambda low: ret_phi.at[t, lax.div(low, 2), lax.rem(low, 2)], back_phi, ret_phi_send, ret_phi_recv)

        pl.when(t < GROUPS - 1)(give_phi)
        last(mean)
        val = jnp.where(mask_val, dot(val_hot, acc_ref[...]), 0.0)
        ret_val[t] = dot_t(peer_m, val).reshape(PEERS, 1, PTS)
        give(lambda low: ret_val.at[t, low], back_val, ret_val_send, ret_val_recv)
        pl.when(t == GROUPS - 1)(give_phi)
        return carry

    lax.fori_loop(0, GROUPS, group, 0)

    for t in range(GROUPS):
        mine = back_val.at[pl.ds(lax.rem(my_x + t, GROUPS) * PEERS, PEERS)]
        pltpu.make_async_copy(mine, mine, ret_val_recv.at[t]).wait()
    owner_col = (iota((PTS, RVES), 1) == target_col).astype(f32)
    vals = dot(owner_col, back_val[:, 0, :])
    vals = jnp.where(iota((PTS, PTS), 1) // 32 == rank_col, vals, 0.0)
    fold = (iota((32, PTS), 1) % 32 == iota((32, PTS), 0)).astype(f32)
    point = dot_t(fold, vals)
    for c in range(3):
        tan_out[c] = point[8 * c + 8:8 * c + 11]

    nodal = gw_ref[0] * point[0:1] + gw_ref[1] * point[1:2] + gw_ref[2] * point[2:3]
    conn = conn_ref[...]
    spread = jnp.zeros((ROWS, PTS), f32)
    for a in range(8):
        spread = spread + jnp.where(conn[a:a + 1] == order_col, nodal[a:a + 1], 0.0)
    spread = jnp.concatenate([spread, jnp.zeros((PTS - ROWS, PTS), f32)], axis=0)
    grid = dot_t(jnp.ones((8, PTS), f32), spread)[0:1]
    halo_src[...] = grid
    turns = [(ds, dr) for ds in (-1, 0, 1) for dr in (-1, 0, 1) if (ds, dr) != (0, 0)]
    copies = [
        pltpu.make_async_remote_copy(
            src_ref=halo_src, dst_ref=halo_dst.at[i], send_sem=halo_send.at[i], recv_sem=halo_recv.at[i],
            device_id=(slab + ds, (left, me, right)[dr + 1]), device_id_type=MESH)
        for i, (ds, dr) in enumerate(turns)]
    for (ds, dr), copy in zip(turns, copies):
        toward(ds, copy.start)

    found = jnp.zeros((2 * PTS, HALF), f32)
    for t in range(GROUPS):
        base = lax.rem(my_x + t, GROUPS) * PEERS
        mine = back_phi.at[pl.ds(base, PEERS)]
        pltpu.make_async_copy(mine, mine, ret_phi_recv.at[t]).wait()
        slot_cols = iota((PTS, PEERS * 8), 1) + base * 8
        hot = jnp.concatenate([(slot_cols == place_col).astype(f32), (slot_cols == place_col + 4).astype(f32)], axis=0)
        found = found + dot(hot, mine[...].reshape(PEERS * 8, HALF))
    pot_out[:, :HALF] = found[:PTS]
    pot_out[:, HALF:] = found[PTS:]

    lane = iota((1, PTS), 1)
    at_i, at_j = lane // 15, lane // 5 % 3
    total = grid
    for i, (ds, dr) in enumerate(turns):
        toward(-ds, copies[i].wait_recv)
        ok = lane < NODES
        if dr != 0:
            ok = ok & (at_i == (0 if dr > 0 else 2)) & ((me > 0) if dr > 0 else (me < RVES - 1))
        if ds != 0:
            ok = ok & (at_j == (0 if ds > 0 else 2)) & ((slab > 0) if ds > 0 else (slab < SLABS - 1))
        shift = (-30 * dr - 10 * ds) % PTS
        moved = pltpu.roll(jnp.broadcast_to(halo_dst[i], (8, PTS)), shift, 1)[0:1]
        total = total + jnp.where(ok, moved, 0.0)
    total = jnp.where(lane < NODES, total, 0.0)
    high, low = parts(jnp.broadcast_to(total, (8, PTS)))
    node_hot = (iota((ROWS, PTS), 0) == order_row).astype(bf16)
    back = mm(high, node_hot, 1) + mm(low, node_hot, 1)
    res_out[...] = back[0:1, :NODES]

    for (ds, dr), copy in zip(turns, copies):
        toward(ds, copy.wait_send)
    for t in range(GROUPS):
        n = PEERS - 1 if t == 0 else PEERS
        pltpu.make_async_copy(send_phi.at[pl.ds(0, n)], send_phi.at[pl.ds(0, n)], out_phi_send.at[t]).wait()
        pltpu.make_async_copy(send_mac.at[pl.ds(0, n)], send_mac.at[pl.ds(0, n)], out_mac_send.at[t]).wait()
        pltpu.make_async_copy(send_phi.at[pl.ds(0, n)], send_phi.at[pl.ds(0, n)], ret_phi_send.at[t]).wait()
        pltpu.make_async_copy(send_mac.at[pl.ds(0, n)], send_mac.at[pl.ds(0, n)], ret_val_send.at[t]).wait()


def on_device(
    macro_field, rve_owner, potential, switch_words, permeability, coercivity, grain_axes,
    hyst_axis, hyst_low, hyst_high, hyst_weight, grad_weights, connectivity, node_order,
):
    vmem = pl.BlockSpec(memory_space=pltpu.VMEM)
    hbm = pl.BlockSpec(memory_space=pltpu.HBM)
    pot, tan, res = pl.pallas_call(
        kernel,
        out_shape=(
            pltpu.VMEM((PTS, 2 * HALF), f32),
            pltpu.VMEM((3, 3, PTS), f32),
            pltpu.VMEM((1, NODES), f32),
        ),
        in_specs=[hbm] * 14,
        out_specs=(vmem, vmem, vmem),
        scratch_shapes=[
            pltpu.VMEM((1, PTS), jnp.int32),
            pltpu.VMEM((3, PTS), f32),
            pltpu.VMEM((PTS, 2 * HALF), f32),
            pltpu.SMEM((3, 4), f32),
            pltpu.SMEM((4,), f32),
            pltpu.SMEM((4,), f32),
            pltpu.SMEM((4,), f32),
            pltpu.VMEM((3, 8, PTS), f32),
            pltpu.VMEM((8, PTS), jnp.int32),
            pltpu.VMEM((1, NODES), jnp.int32),
            pltpu.SemaphoreType.DMA((10,)),
            pltpu.VMEM((GROUPS, SLOTS, 2 * HALF), jnp.int32),
            pltpu.VMEM((GROUPS, SLOTS, 2 * HALF), f32),
            pltpu.VMEM((GROUPS, SLOTS, 2 * HALF), f32),
            pltpu.VMEM((GROUPS, 3, SLOTS, 2 * HALF), f32),
            pltpu.VMEM((4, 8, 8, PTS), jnp.int32),
            pltpu.VMEM((N_FIELDS, 4, 8, 8, PTS), f32),
            pltpu.VMEM((RVES, 8, HALF), f32),
            pltpu.VMEM((RVES, 1, PTS), f32),
            pltpu.VMEM((GROUPS, PEERS, 8, HALF), f32),
            pltpu.VMEM((GROUPS, PEERS, 1, PTS), f32),
            pltpu.VMEM((GROUPS, PEERS // 2, 2, 8, HALF), f32),
            pltpu.VMEM((GROUPS, PEERS, 1, PTS), f32),
            pltpu.VMEM((RVES, 8, HALF), f32),
            pltpu.VMEM((RVES, 1, PTS), f32),
            pltpu.VMEM((96, PTS), f32),
            pltpu.VMEM((1, PTS), f32),
            pltpu.VMEM((8, 1, PTS), f32),
            pltpu.SemaphoreType.DMA((4, GROUPS)),
        ] + [pltpu.SemaphoreType.DMA((GROUPS,))] * 8 + [pltpu.SemaphoreType.DMA((8,))] * 2,
        compiler_params=pltpu.CompilerParams(
            collective_id=0, has_side_effects=True, vmem_limit_bytes=60 * 1024 * 1024),
    )(rve_owner.reshape(1, PTS), macro_field, potential, switch_words, permeability, coercivity, grain_axes,
      hyst_axis, hyst_low, hyst_high, hyst_weight, grad_weights, connectivity, node_order.reshape(1, NODES))
    return pot, tan, res.reshape(NODES)


def solution(mesh):
    return jax.shard_map(
        on_device,
        mesh=mesh,
        in_specs=(
            P(None, ("slab", "rve")),
            P(("slab", "rve"), None),
            P(("slab", "rve"), None),
            P(("slab", "rve"), None),
            P(("slab", "rve"), None),
            P(("slab", "rve"), None),
            P(None, ("slab", "rve"), None),
            P(),
            P(),
            P(),
            P(),
            P(None, None, ("slab", "rve")),
            P(None, ("slab", "rve")),
            P(("slab", "rve")),
        ),
        out_specs=(P(("slab", "rve"), None), P(None, None, ("slab", "rve")), P(("slab", "rve"))),
        check_vma=False,
    )
```

```python
import jax
import jax.numpy as jnp
from jax import lax
from jax.experimental import pallas as pl
from jax.experimental.pallas import tpu as pltpu
from jax.sharding import PartitionSpec as P

MESH = pl.DeviceIdType.MESH
f32 = jnp.float32
bf16 = jnp.bfloat16

GROUPS = 4
PEERS = 16
CAP = 4
SLOTS = PEERS * CAP
RVES = GROUPS * PEERS
SLABS = 8
PTS = 128
HALF = 256
NODES = 45
ROWS = 48
UNROLL = (7, 7, 8, 8)
HOLD = 1

PERM = 0
GRAIN = 1
TH = 4
PG = 8
AIJ = 11
N_HELD = 17
PHI = 0
PSI = 3
N_FIELDS = 9
PAIRS = ((0, 0), (0, 1), (0, 2), (1, 1), (1, 2), (2, 2))


def iota(shape, dim):
    return lax.broadcasted_iota(jnp.int32, shape, dim)


def parts(data):
    high = data.astype(bf16)
    return high, (data - high.astype(f32)).astype(bf16)


def mm(a, b, dim):
    return lax.dot_general(a, b, (((1,), (dim,)), ((), ())), preferred_element_type=f32)


def dot(hot, data):
    high, low = parts(data)
    hot = hot.astype(bf16)
    return mm(hot, high, 0) + mm(hot, low, 0)


def dot_t(hot, data):
    high, low = parts(data)
    hot = hot.astype(bf16)
    return mm(hot, high, 1) + mm(hot, low, 1)


def swap(v):
    return pltpu.roll(v, 64, v.ndim - 1)


def next_x(v):
    return jnp.concatenate([v[1:], swap(v[:1])], axis=0)


def prev_x(v):
    return jnp.concatenate([swap(v[3:]), v[:3]], axis=0)


def next_z(v):
    return pltpu.roll(v, 7, 1)


def prev_z(v):
    return pltpu.roll(v, 1, 1)


def recip(v):
    r = pl.reciprocal(v, approx=True)
    return r * (2.0 - v * r)


def sum_x(v):
    return (v[0] + v[1]) + (v[2] + v[3])


def to_rows(recv):
    n = recv.shape[-1]
    pairs = recv.reshape(8, 2, 8, n)
    even, odd = pairs[:, 0], pairs[:, 1]
    first = iota((8, 8, n), 1) < 4
    low = jnp.where(first, even, pltpu.roll(odd, 4, 1))
    high = jnp.where(first, pltpu.roll(even, 4, 1), odd)
    return jnp.concatenate([low.reshape(64, n), high.reshape(64, n)], axis=0)


def kernel(
    owner_hbm, macro_hbm, pot_hbm, words_hbm, perm_hbm, coer_hbm, grain_hbm,
    axis_hbm, low_hbm, high_hbm, weight_hbm, gw_hbm, conn_hbm, order_hbm,
    pot_out, tan_out, res_out,
    owner_ref, macro_ref, pot_ref, axis_ref, low_ref, high_ref, weight_ref, gw_ref, conn_ref, order_ref, early_sem,
    nat_words, nat_perm, nat_coer, nat_grain, words_t, coer_t, held, fields,
    send_phi, send_mac, recv_phi, recv_mac, ret_phi, ret_val, back_phi, back_val,
    acc_ref, means, halo_src, halo_dst,
    load_sem, out_phi_send, out_phi_recv, out_mac_send, out_mac_recv,
    ret_phi_send, ret_phi_recv, ret_val_send, ret_val_recv, halo_send, halo_recv,
):
    me = lax.axis_index("rve")
    slab = lax.axis_index("slab")
    my_x = lax.div(me, PEERS)
    my_low = lax.rem(me, PEERS)
    right, left = lax.rem(me + 1, RVES), lax.rem(me + RVES - 1, RVES)

    early = [
        pltpu.make_async_copy(src, dst, early_sem.at[i])
        for i, (src, dst) in enumerate((
            (owner_hbm, owner_ref), (pot_hbm, pot_ref), (macro_hbm, macro_ref), (axis_hbm, axis_ref),
            (low_hbm, low_ref), (high_hbm, high_ref), (weight_hbm, weight_ref), (gw_hbm, gw_ref),
            (conn_hbm, conn_ref), (order_hbm, order_ref)))
    ]
    for copy in early[:3]:
        copy.start()

    barrier = pltpu.get_barrier_semaphore()

    def greet(i, carry):
        peer = lax.rem(me + i, RVES)
        pl.semaphore_signal(barrier, inc=1, device_id=(slab, peer), device_id_type=MESH)
        return carry

    lax.fori_loop(1, RVES, greet, 0, unroll=7)

    def toward(ds, action):
        if ds == 0:
            action()
        else:
            pl.when((slab > 0) if ds < 0 else (slab < SLABS - 1))(action)

    for ds in (-1, 1):
        def hail(ds=ds):
            for r in (left, me, right):
                pl.semaphore_signal(barrier, inc=1, device_id=(slab + ds, r), device_id_type=MESH)

        toward(ds, hail)

    def loads(t):
        rows = pl.ds(lax.rem(my_x - t + GROUPS, GROUPS) * SLOTS, SLOTS)
        return (
            pltpu.make_async_copy(words_hbm.at[rows], nat_words.at[t], load_sem.at[0, t]),
            pltpu.make_async_copy(perm_hbm.at[rows], nat_perm.at[t], load_sem.at[1, t]),
            pltpu.make_async_copy(coer_hbm.at[rows], nat_coer.at[t], load_sem.at[2, t]),
            pltpu.make_async_copy(grain_hbm.at[:, rows], nat_grain.at[t], load_sem.at[3, t]),
        )

    for copy in early[3:]:
        copy.start()
    for t in range(GROUPS):
        for copy in loads(t):
            copy.start()

    early[0].wait()
    target_row = owner_ref[...]
    target_rows = jnp.broadcast_to(target_row.astype(f32), (PTS, PTS))
    target_cols = target_rows.T
    same = target_rows == target_cols
    q_row, q_col = iota((PTS, PTS), 1), iota((PTS, PTS), 0)
    rank_row = jnp.sum(jnp.where(same & (q_col < q_row), 1.0, 0.0), axis=0, keepdims=True).astype(jnp.int32)
    rank_col = jnp.sum(jnp.where(same & (q_row < q_col), 1.0, 0.0), axis=1, keepdims=True).astype(jnp.int32)
    target_col = target_cols[:, :1].astype(jnp.int32)
    place_row = target_row * 8 + rank_row
    place_col = target_col * 8 + rank_col

    early[1].wait()
    early[2].wait()
    halves = parts(jnp.concatenate([pot_ref[:, :HALF], pot_ref[:, HALF:]], axis=0))

    n_rows = iota((PTS, PTS), 0)
    comp = n_rows // CAP
    spread = jnp.where(comp == 0, macro_ref[0:1], jnp.where(comp == 1, macro_ref[1:2], macro_ref[2:3]))
    spread = jnp.where((comp < 3) & (n_rows % CAP == rank_row), spread, 0.0)
    owner_hot = (iota((RVES, PTS), 0) == target_row).astype(f32)
    send_mac[...] = dot_t(owner_hot, spread).reshape(RVES, 1, PTS)

    sides = lax.div(slab + SLABS - 1, SLABS) + lax.div(2 * SLABS - 2 - slab, SLABS)
    pl.semaphore_wait(barrier, RVES - 1 + 3 * sides)

    def partner(i):
        k = lax.div(i, 2)
        step = lax.div(k + 1, 2) * (2 * lax.rem(k, 2) - 1)
        return lax.rem(my_low + 2 * step + PEERS + lax.rem(i, 2) * (1 - 2 * lax.rem(my_low, 2)), PEERS)

    def issue(t, peer_x, start, start_local):
        def one(i, carry):
            low = partner(i)
            start(low, peer_x * PEERS + low)
            return carry

        if isinstance(t, int):
            (start_local if t == 0 else start)(my_low, peer_x * PEERS + my_low)
        else:
            @pl.when(t == 0)
            def _():
                start_local(my_low, me)

            @pl.when(t > 0)
            def _():
                start(my_low, peer_x * PEERS + my_low)

        lax.fori_loop(1, PEERS, one, 0, unroll=5)

    def send(t):
        issue(
            t, lax.rem(my_x + t, GROUPS),
            lambda low, peer: pltpu.make_async_remote_copy(
                src_ref=send_phi.at[peer], dst_ref=recv_phi.at[t, my_low],
                send_sem=out_phi_send.at[t], recv_sem=out_phi_recv.at[t],
                device_id=(slab, peer), device_id_type=MESH).start(),
            lambda low, peer: pltpu.make_async_copy(
                send_phi.at[peer], recv_phi.at[t, my_low], out_phi_recv.at[t]).start())

    def send_field(t):
        issue(
            t, lax.rem(my_x + t, GROUPS),
            lambda low, peer: pltpu.make_async_remote_copy(
                src_ref=send_mac.at[peer], dst_ref=recv_mac.at[t, my_low],
                send_sem=out_mac_send.at[t], recv_sem=out_mac_recv.at[t],
                device_id=(slab, peer), device_id_type=MESH).start(),
            lambda low, peer: pltpu.make_async_copy(
                send_mac.at[peer], recv_mac.at[t, my_low], out_mac_recv.at[t]).start())

    slot_rows = iota((PEERS * 8, PTS), 0)
    for t in range(GROUPS):
        base = lax.rem(my_x + t, GROUPS) * PEERS
        rows = slot_rows + base * 8
        hot = jnp.concatenate([(rows == place_row).astype(f32), (rows == place_row + 4).astype(f32)], axis=1)
        hot = hot.astype(bf16)
        send_phi[pl.ds(base, PEERS)] = (mm(hot, halves[0], 0) + mm(hot, halves[1], 0)).reshape(PEERS, 8, HALF)
        send(t)
        if t == 0:
            for other in range(GROUPS):
                send_field(other)
    for copy in early[3:]:
        copy.wait()

    order_row = jnp.sum(jnp.where(iota((PTS, NODES), 0) == iota((PTS, NODES), 1), order_ref[...].astype(f32), 0.0),
                        axis=1, keepdims=True)
    order_cols = jnp.where(iota((PTS, PTS), 0) < NODES, jnp.broadcast_to(order_row, (PTS, PTS)), -1.0)
    order_row = order_cols.T[:1].astype(jnp.int32)
    order_col = order_cols[:ROWS].astype(jnp.int32)

    lane_peer = iota((PTS, PEERS), 0) // CAP % PEERS
    peer_t = (lane_peer == iota((PTS, PEERS), 1)).astype(f32)
    peer_m = (iota((PEERS, PTS), 1) // CAP % PEERS == iota((PEERS, PTS), 0)).astype(f32)
    mask_mac = iota((PTS, PTS), 0) % CAP == iota((PTS, PTS), 1) % CAP
    comp_m = (iota((8, PTS), 1) // CAP == iota((8, PTS), 0)).astype(f32)
    val_n = iota((PTS, 96), 0) % 32
    val_k = iota((PTS, 96), 1) // 8
    val_hot = jnp.where(
        jnp.where(val_k < 3, val_k, (val_k // 3) * 8 + val_k % 3) == val_n, 1.0 / 512.0, 0.0)
    mask_val = iota((PTS, PTS), 0) // 32 == iota((PTS, PTS), 1) % CAP

    axis2 = [[2.0 * axis_ref[c, k] for k in range(4)] for c in range(3)]
    mag_w = [[weight_ref[k] * axis_ref[c, k] for k in range(4)] for c in range(3)]
    pair_w = [[2.0 * weight_ref[k] * axis_ref[a, k] * axis_ref[b, k] for k in range(4)] for a, b in PAIRS]
    low2 = [2.0 * low_ref[k] for k in range(4)]
    high2 = [2.0 * high_ref[k] for k in range(4)]

    def evaluate(t, y, version, mean):
        now = fields[PHI + version, :, y]
        y_next = fields[PHI + version, :, lax.rem(y + 1, 8)]
        h = [mean[0] + (next_x(now) - now), mean[1] + (y_next - now), mean[2] + (next_z(now) - now)]
        g = [held[t, GRAIN + c, :, y] * h[c] for c in range(3)]
        s = []
        for k in range(4):
            arg = axis2[0][k] * g[0] + axis2[1][k] * g[1] + axis2[2][k] * g[2] - held[t, TH + k, :, y]
            s.append(jnp.tanh(arg))
        slope = [1.0 - v * v for v in s]
        perm = held[t, PERM, :, y]
        flux = []
        for c in range(3):
            mag = mag_w[c][0] * s[0] + mag_w[c][1] * s[1] + mag_w[c][2] * s[2] + mag_w[c][3] * s[3]
            flux.append(perm * h[c] + held[t, PG + c, :, y] * mag)
        stiff = {}
        for i, pair in enumerate(PAIRS):
            w = pair_w[i]
            total = w[0] * slope[0] + w[1] * slope[1] + w[2] * slope[2] + w[3] * slope[3]
            v = held[t, AIJ + i, :, y] * total
            if pair[0] == pair[1]:
                v = v + perm
            stiff[pair] = v
            stiff[pair[::-1]] = v
        return now, flux, stiff

    def sweep_body(t, y, first, mean, carry):
        now, flux, stiff = evaluate(t, y, 0 if first else 1, mean)
        if first:
            lin = stiff
        else:
            lin = {}
            psi = [fields[PSI + d, :, y] for d in range(3)]
            psi_y = [fields[PSI + d, :, lax.rem(y + 1, 8)] for d in range(3)]
            for d in range(3):
                grad = [next_x(psi[d]) - psi[d], psi_y[d] - psi[d], next_z(psi[d]) - psi[d]]
                grad[d] = grad[d] + 1.0
                for c in range(3):
                    lin[c, d] = stiff[c, 0] * grad[0] + stiff[c, 1] * grad[1] + stiff[c, 2] * grad[2]
        nxt = (flux[1], stiff[1, 1], lin[1, 0], lin[1, 1], lin[1, 2])
        cross = stiff[0, 1] + stiff[0, 2] + stiff[1, 2]
        weight = (stiff[0, 0] + stiff[1, 1] + stiff[2, 2] + (cross + cross)
                  + prev_x(stiff[0, 0]) + prev_z(stiff[2, 2]))
        force = (flux[0] - prev_x(flux[0])) + flux[1] + (flux[2] - prev_z(flux[2]))
        forces = [(lin[0, d] - prev_x(lin[0, d])) + lin[1, d] + (lin[2, d] - prev_z(lin[2, d])) for d in range(3)]
        if carry is not None:
            force, weight, forces = close(force, weight, forces, carry)
        return nxt, (force, weight, forces)

    def close(force, weight, forces, carry):
        return force - carry[0], weight + carry[1], [forces[d] - carry[2 + d] for d in range(3)]

    def apply(y, first, sums):
        force, weight, forces = sums
        inv = recip(1.5 * weight)
        old, new = (0, 1) if first else (1, 2)
        fields[PHI + new, :, y] = fields[PHI + old, :, y] + force * inv
        for d in range(3):
            step = forces[d] * inv
            if not first:
                step = fields[PSI + d, :, y] + step
            fields[PSI + (0 if first else 3) + d, :, y] = step

    def sweep(t, first, mean):
        carry, (force, weight, forces) = sweep_body(t, 0, first, mean, None)

        def step(y, carry):
            nxt, sums = sweep_body(t, y, first, mean, carry)
            apply(y, first, sums)
            return nxt

        carry = lax.fori_loop(1, 8, step, carry, unroll=UNROLL[0 if first else 1])
        apply(0, first, close(force, weight, forces, carry))

    def last(t, mean):
        def step(y, carry):
            prev, acc = carry
            now, flux, stiff = evaluate(t, y, 2, mean)
            psi = [fields[PSI + 3 + d, :, y] for d in range(3)]
            acc = list(acc)
            for c in range(3):
                acc[c] = acc[c] + sum_x(flux[c])
            for i, pair in enumerate(PAIRS):
                acc[3 + i] = acc[3 + i] + sum_x(stiff[pair])
            for c in range(3):
                div = ((stiff[0, c] - prev_x(stiff[0, c])) + (stiff[1, c] - prev[c])
                       + (stiff[2, c] - prev_z(stiff[2, c])))
                for d in range(3):
                    acc[9 + 3 * c + d] = acc[9 + 3 * c + d] + sum_x(div * psi[d])
            return (stiff[0, 1], stiff[1, 1], stiff[1, 2]), tuple(acc)

        zero = jnp.zeros((4, 8, PTS), f32)
        flat = jnp.zeros((8, PTS), f32)
        prev, acc = lax.fori_loop(0, 8, step, ((zero,) * 3, (flat,) * 18), unroll=UNROLL[2])
        psi = [fields[PSI + 3 + d, :, 0] for d in range(3)]
        for c in range(3):
            acc_ref[t, 8 * c:8 * c + 8] = acc[c]
            for d in range(3):
                pair = PAIRS.index((min(c, d), max(c, d)))
                k = 3 + 3 * c + d
                acc_ref[t, 8 * k:8 * k + 8] = acc[3 + pair] - acc[9 + 3 * c + d] + sum_x(prev[c] * psi[d])

    def turn(nat, h):
        a = nat[:, h * PTS:(h + 1) * PTS]
        b = nat[:, HALF + h * PTS:HALF + (h + 1) * PTS]
        return jnp.concatenate([a, b], axis=0).T.reshape(2, 8, 8, PTS)

    def ahead(t, carry):
        for copy in loads(t):
            copy.wait()
        for h in range(2):
            xs = slice(2 * h, 2 * h + 2)
            words_t[xs] = turn(nat_words[t], h)
            coer_t[xs] = turn(nat_coer[t], h)
            held[t, PERM, xs] = turn(nat_perm[t], h)
            for c in range(3):
                held[t, GRAIN + c, xs] = turn(nat_grain[t, c], h)

        def prepare(y, inner):
            words = words_t[:, y]
            coer = coer_t[:, y]
            for k in range(4):
                up = jnp.bitwise_and(words, 1 << k) != 0
                held[t, TH + k, :, y] = coer * jnp.where(up, low2[k], high2[k])
            perm = held[t, PERM, :, y]
            grain = [held[t, GRAIN + c, :, y] for c in range(3)]
            pg = [perm * grain[c] for c in range(3)]
            for c in range(3):
                held[t, PG + c, :, y] = pg[c]
            for i, (a, b) in enumerate(PAIRS):
                held[t, AIJ + i, :, y] = pg[a] * grain[b]
            return inner

        lax.fori_loop(0, 8, prepare, 0, unroll=UNROLL[3])
        return carry

    lax.fori_loop(0, GROUPS, ahead, 0)
    for t in range(GROUPS):
        pltpu.make_async_copy(recv_mac.at[t], recv_mac.at[t], out_mac_recv.at[t]).wait()
        mac = dot(peer_t, recv_mac[t, :, 0, :])
        means[t] = dot_t(comp_m, jnp.where(mask_mac, mac, 0.0))
    def group(t, carry):
        pltpu.make_async_copy(recv_phi.at[t], recv_phi.at[t], out_phi_recv.at[t]).wait()
        rows = to_rows(recv_phi[t])
        for h in range(2):
            fields[PHI, 2 * h:2 * h + 2] = rows[:, h * PTS:(h + 1) * PTS].T.reshape(2, 8, 8, PTS)
        mean = [jnp.broadcast_to(means[t, c:c + 1], (8, PTS))[None] for c in range(3)]

        sweep(t, True, mean)
        sweep(t, False, mean)

        first = iota((8, 8, PTS), 1) < 4
        for h in range(2):
            block = fields[PHI + 2, 2 * h:2 * h + 2].reshape(PTS, PTS).T.reshape(2, 8, 8, PTS)
            low, high = block[0], block[1]
            cols = slice(h * PTS, (h + 1) * PTS)
            ret_phi[t, :, 0, :, cols] = jnp.where(first, low, pltpu.roll(high, 4, 1))
            ret_phi[t, :, 1, :, cols] = jnp.where(first, pltpu.roll(low, 4, 1), high)

        @pl.when(t < GROUPS - HOLD)
        def _():
            give_phi(t)

        last(t, mean)
        return carry

    def give(t, src, dst, send_sem, recv_sem):
        issue(
            t, lax.rem(my_x - t + GROUPS, GROUPS),
            lambda low, peer: pltpu.make_async_remote_copy(
                src_ref=src(low), dst_ref=dst.at[me], send_sem=send_sem.at[t], recv_sem=recv_sem.at[t],
                device_id=(slab, peer), device_id_type=MESH).start(),
            lambda low, peer: pltpu.make_async_copy(src(low), dst.at[me], recv_sem.at[t]).start())

    def give_phi(t):
        give(t, lambda low: ret_phi.at[t, lax.div(low, 2), lax.rem(low, 2)], back_phi, ret_phi_send, ret_phi_recv)

    lax.fori_loop(0, GROUPS, group, 0)
    for t in range(GROUPS):
        val = jnp.where(mask_val, dot(val_hot, acc_ref[t]), 0.0)
        ret_val[t] = dot_t(peer_m, val).reshape(PEERS, 1, PTS)
    for t in range(GROUPS):
        give(t, lambda low, t=t: ret_val.at[t, low], back_val, ret_val_send, ret_val_recv)
    for t in range(GROUPS - HOLD, GROUPS):
        give_phi(t)

    for t in range(GROUPS):
        mine = back_val.at[pl.ds(lax.rem(my_x + t, GROUPS) * PEERS, PEERS)]
        pltpu.make_async_copy(mine, mine, ret_val_recv.at[t]).wait()
    owner_col = (iota((PTS, RVES), 1) == target_col).astype(f32)
    vals = dot(owner_col, back_val[:, 0, :])
    vals = jnp.where(iota((PTS, PTS), 1) // 32 == rank_col, vals, 0.0)
    fold = (iota((32, PTS), 1) % 32 == iota((32, PTS), 0)).astype(f32)
    point = dot_t(fold, vals)
    for c in range(3):
        tan_out[c] = point[8 * c + 8:8 * c + 11]

    nodal = gw_ref[0] * point[0:1] + gw_ref[1] * point[1:2] + gw_ref[2] * point[2:3]
    conn = conn_ref[...]
    spread = jnp.zeros((ROWS, PTS), f32)
    for a in range(8):
        spread = spread + jnp.where(conn[a:a + 1] == order_col, nodal[a:a + 1], 0.0)
    spread = jnp.concatenate([spread, jnp.zeros((PTS - ROWS, PTS), f32)], axis=0)
    grid = dot_t(jnp.ones((8, PTS), f32), spread)[0:1]
    halo_src[...] = grid
    turns = [(ds, dr) for ds in (-1, 0, 1) for dr in (-1, 0, 1) if (ds, dr) != (0, 0)]
    copies = [
        pltpu.make_async_remote_copy(
            src_ref=halo_src, dst_ref=halo_dst.at[i], send_sem=halo_send.at[i], recv_sem=halo_recv.at[i],
            device_id=(slab + ds, (left, me, right)[dr + 1]), device_id_type=MESH)
        for i, (ds, dr) in enumerate(turns)]
    for (ds, dr), copy in zip(turns, copies):
        toward(ds, copy.start)

    found = jnp.zeros((2 * PTS, HALF), f32)
    for t in range(GROUPS):
        base = lax.rem(my_x + t, GROUPS) * PEERS
        mine = back_phi.at[pl.ds(base, PEERS)]
        pltpu.make_async_copy(mine, mine, ret_phi_recv.at[t]).wait()
        slot_cols = iota((PTS, PEERS * 8), 1) + base * 8
        hot = jnp.concatenate([(slot_cols == place_col).astype(f32), (slot_cols == place_col + 4).astype(f32)], axis=0)
        found = found + dot(hot, mine[...].reshape(PEERS * 8, HALF))
    pot_out[:, :HALF] = found[:PTS]
    pot_out[:, HALF:] = found[PTS:]

    lane = iota((1, PTS), 1)
    at_i, at_j = lane // 15, lane // 5 % 3
    total = grid
    for i, (ds, dr) in enumerate(turns):
        toward(-ds, copies[i].wait_recv)
        ok = lane < NODES
        if dr != 0:
            ok = ok & (at_i == (0 if dr > 0 else 2)) & ((me > 0) if dr > 0 else (me < RVES - 1))
        if ds != 0:
            ok = ok & (at_j == (0 if ds > 0 else 2)) & ((slab > 0) if ds > 0 else (slab < SLABS - 1))
        shift = (-30 * dr - 10 * ds) % PTS
        moved = pltpu.roll(jnp.broadcast_to(halo_dst[i], (8, PTS)), shift, 1)[0:1]
        total = total + jnp.where(ok, moved, 0.0)
    total = jnp.where(lane < NODES, total, 0.0)
    high, low = parts(jnp.broadcast_to(total, (8, PTS)))
    node_hot = (iota((ROWS, PTS), 0) == order_row).astype(bf16)
    back = mm(high, node_hot, 1) + mm(low, node_hot, 1)
    res_out[...] = back[0:1, :NODES]

    for (ds, dr), copy in zip(turns, copies):
        toward(ds, copy.wait_send)
    for t in range(GROUPS):
        n = PEERS - 1 if t == 0 else PEERS
        pltpu.make_async_copy(send_phi.at[pl.ds(0, n)], send_phi.at[pl.ds(0, n)], out_phi_send.at[t]).wait()
        pltpu.make_async_copy(send_mac.at[pl.ds(0, n)], send_mac.at[pl.ds(0, n)], out_mac_send.at[t]).wait()
        pltpu.make_async_copy(send_phi.at[pl.ds(0, n)], send_phi.at[pl.ds(0, n)], ret_phi_send.at[t]).wait()
        pltpu.make_async_copy(send_mac.at[pl.ds(0, n)], send_mac.at[pl.ds(0, n)], ret_val_send.at[t]).wait()


def on_device(
    macro_field, rve_owner, potential, switch_words, permeability, coercivity, grain_axes,
    hyst_axis, hyst_low, hyst_high, hyst_weight, grad_weights, connectivity, node_order,
):
    vmem = pl.BlockSpec(memory_space=pltpu.VMEM)
    hbm = pl.BlockSpec(memory_space=pltpu.HBM)
    pot, tan, res = pl.pallas_call(
        kernel,
        out_shape=(
            pltpu.VMEM((PTS, 2 * HALF), f32),
            pltpu.VMEM((3, 3, PTS), f32),
            pltpu.VMEM((1, NODES), f32),
        ),
        in_specs=[hbm] * 14,
        out_specs=(vmem, vmem, vmem),
        scratch_shapes=[
            pltpu.VMEM((1, PTS), jnp.int32),
            pltpu.VMEM((3, PTS), f32),
            pltpu.VMEM((PTS, 2 * HALF), f32),
            pltpu.SMEM((3, 4), f32),
            pltpu.SMEM((4,), f32),
            pltpu.SMEM((4,), f32),
            pltpu.SMEM((4,), f32),
            pltpu.VMEM((3, 8, PTS), f32),
            pltpu.VMEM((8, PTS), jnp.int32),
            pltpu.VMEM((1, NODES), jnp.int32),
            pltpu.SemaphoreType.DMA((10,)),
            pltpu.VMEM((GROUPS, SLOTS, 2 * HALF), jnp.int32),
            pltpu.VMEM((GROUPS, SLOTS, 2 * HALF), f32),
            pltpu.VMEM((GROUPS, SLOTS, 2 * HALF), f32),
            pltpu.VMEM((GROUPS, 3, SLOTS, 2 * HALF), f32),
            pltpu.VMEM((4, 8, 8, PTS), jnp.int32),
            pltpu.VMEM((4, 8, 8, PTS), f32),
            pltpu.VMEM((GROUPS, N_HELD, 4, 8, 8, PTS), f32),
            pltpu.VMEM((N_FIELDS, 4, 8, 8, PTS), f32),
            pltpu.VMEM((RVES, 8, HALF), f32),
            pltpu.VMEM((RVES, 1, PTS), f32),
            pltpu.VMEM((GROUPS, PEERS, 8, HALF), f32),
            pltpu.VMEM((GROUPS, PEERS, 1, PTS), f32),
            pltpu.VMEM((GROUPS, PEERS // 2, 2, 8, HALF), f32),
            pltpu.VMEM((GROUPS, PEERS, 1, PTS), f32),
            pltpu.VMEM((RVES, 8, HALF), f32),
            pltpu.VMEM((RVES, 1, PTS), f32),
            pltpu.VMEM((GROUPS, 96, PTS), f32),
            pltpu.VMEM((GROUPS, 8, PTS), f32),
            pltpu.VMEM((1, PTS), f32),
            pltpu.VMEM((8, 1, PTS), f32),
            pltpu.SemaphoreType.DMA((4, GROUPS)),
        ] + [pltpu.SemaphoreType.DMA((GROUPS,))] * 8 + [pltpu.SemaphoreType.DMA((8,))] * 2,
        compiler_params=pltpu.CompilerParams(
            collective_id=0, has_side_effects=True, vmem_limit_bytes=60 * 1024 * 1024),
    )(rve_owner.reshape(1, PTS), macro_field, potential, switch_words, permeability, coercivity, grain_axes,
      hyst_axis, hyst_low, hyst_high, hyst_weight, grad_weights, connectivity, node_order.reshape(1, NODES))
    return pot, tan, res.reshape(NODES)


def solution(mesh):
    return jax.shard_map(
        on_device,
        mesh=mesh,
        in_specs=(
            P(None, ("slab", "rve")),
            P(("slab", "rve"), None),
            P(("slab", "rve"), None),
            P(("slab", "rve"), None),
            P(("slab", "rve"), None),
            P(("slab", "rve"), None),
            P(None, ("slab", "rve"), None),
            P(),
            P(),
            P(),
            P(),
            P(None, None, ("slab", "rve")),
            P(None, ("slab", "rve")),
            P(("slab", "rve")),
        ),
        out_specs=(P(("slab", "rve"), None), P(None, None, ("slab", "rve")), P(("slab", "rve"))),
        check_vma=False,
    )
```

```python
import jax
import jax.numpy as jnp
from jax import lax
from jax.experimental import pallas as pl
from jax.experimental.pallas import tpu as pltpu
from jax.sharding import PartitionSpec as P

MESH = pl.DeviceIdType.MESH
f32 = jnp.float32
bf16 = jnp.bfloat16

GROUPS = 4
PEERS = 16
CAP = 4
SLOTS = PEERS * CAP
RVES = GROUPS * PEERS
SLABS = 8
PTS = 128
HALF = 256
NODES = 45
ROWS = 48
UNROLL = (7, 7, 8, 8)
HOLD = 1

PERM = 0
GRAIN = 1
TH = 4
PG = 8
AIJ = 11
N_HELD = 17
PHI = 0
PSI = 3
N_FIELDS = 9
PAIRS = ((0, 0), (0, 1), (0, 2), (1, 1), (1, 2), (2, 2))


def iota(shape, dim):
    return lax.broadcasted_iota(jnp.int32, shape, dim)


def parts(data):
    high = data.astype(bf16)
    return high, (data - high.astype(f32)).astype(bf16)


def mm(a, b, dim):
    return lax.dot_general(a, b, (((1,), (dim,)), ((), ())), preferred_element_type=f32)


def dot(hot, data):
    high, low = parts(data)
    hot = hot.astype(bf16)
    return mm(hot, high, 0) + mm(hot, low, 0)


def dot_t(hot, data):
    high, low = parts(data)
    hot = hot.astype(bf16)
    return mm(hot, high, 1) + mm(hot, low, 1)


def swap(v):
    return pltpu.roll(v, 64, v.ndim - 1)


def next_x(v):
    return jnp.concatenate([v[1:], swap(v[:1])], axis=0)


def prev_x(v):
    return jnp.concatenate([swap(v[3:]), v[:3]], axis=0)


def next_z(v):
    return pltpu.roll(v, 7, 1)


def prev_z(v):
    return pltpu.roll(v, 1, 1)


def recip(v):
    r = pl.reciprocal(v, approx=True)
    return r * (2.0 - v * r)


def sum_x(v):
    return (v[0] + v[1]) + (v[2] + v[3])


def to_rows(recv):
    n = recv.shape[-1]
    pairs = recv.reshape(8, 2, 8, n)
    even, odd = pairs[:, 0], pairs[:, 1]
    first = iota((8, 8, n), 1) < 4
    low = jnp.where(first, even, pltpu.roll(odd, 4, 1))
    high = jnp.where(first, pltpu.roll(even, 4, 1), odd)
    return jnp.concatenate([low.reshape(64, n), high.reshape(64, n)], axis=0)


def kernel(
    owner_hbm, macro_hbm, pot_hbm, words_hbm, perm_hbm, coer_hbm, grain_hbm,
    axis_hbm, low_hbm, high_hbm, weight_hbm, gw_hbm, conn_hbm, order_hbm,
    pot_out, tan_out, res_out,
    owner_ref, macro_ref, pot_ref, axis_ref, low_ref, high_ref, weight_ref, gw_ref, conn_ref, order_ref, early_sem,
    nat_words, nat_perm, nat_coer, nat_grain, words_t, coer_t, held, fields,
    send_phi, send_mac, recv_phi, recv_mac, ret_phi, ret_val, back_phi, back_val,
    acc_ref, means, halo_src, halo_dst,
    load_sem, out_phi_send, out_phi_recv, out_mac_send, out_mac_recv,
    ret_phi_send, ret_phi_recv, ret_val_send, ret_val_recv, halo_send, halo_recv,
):
    me = lax.axis_index("rve")
    slab = lax.axis_index("slab")
    my_x = lax.div(me, PEERS)
    my_low = lax.rem(me, PEERS)
    right, left = lax.rem(me + 1, RVES), lax.rem(me + RVES - 1, RVES)

    early = [
        pltpu.make_async_copy(src, dst, early_sem.at[i])
        for i, (src, dst) in enumerate((
            (owner_hbm, owner_ref), (pot_hbm, pot_ref), (macro_hbm, macro_ref), (axis_hbm, axis_ref),
            (low_hbm, low_ref), (high_hbm, high_ref), (weight_hbm, weight_ref), (gw_hbm, gw_ref),
            (conn_hbm, conn_ref), (order_hbm, order_ref)))
    ]
    for copy in early[:3]:
        copy.start()

    barrier = pltpu.get_barrier_semaphore()

    def greet(i, carry):
        peer = lax.rem(me + i, RVES)
        pl.semaphore_signal(barrier, inc=1, device_id=(slab, peer), device_id_type=MESH)
        return carry

    lax.fori_loop(1, RVES, greet, 0, unroll=7)

    def toward(ds, action):
        if ds == 0:
            action()
        else:
            pl.when((slab > 0) if ds < 0 else (slab < SLABS - 1))(action)

    for ds in (-1, 1):
        def hail(ds=ds):
            for r in (left, me, right):
                pl.semaphore_signal(barrier, inc=1, device_id=(slab + ds, r), device_id_type=MESH)

        toward(ds, hail)

    def loads(t):
        rows = pl.ds(lax.rem(my_x - t + GROUPS, GROUPS) * SLOTS, SLOTS)
        return (
            pltpu.make_async_copy(words_hbm.at[rows], nat_words.at[t], load_sem.at[0, t]),
            pltpu.make_async_copy(perm_hbm.at[rows], nat_perm.at[t], load_sem.at[1, t]),
            pltpu.make_async_copy(coer_hbm.at[rows], nat_coer.at[t], load_sem.at[2, t]),
            pltpu.make_async_copy(grain_hbm.at[:, rows], nat_grain.at[t], load_sem.at[3, t]),
        )

    for copy in early[3:]:
        copy.start()

    early[0].wait()
    target_row = owner_ref[...]
    target_rows = jnp.broadcast_to(target_row.astype(f32), (PTS, PTS))
    target_cols = target_rows.T
    same = target_rows == target_cols
    q_row, q_col = iota((PTS, PTS), 1), iota((PTS, PTS), 0)
    rank_row = jnp.sum(jnp.where(same & (q_col < q_row), 1.0, 0.0), axis=0, keepdims=True).astype(jnp.int32)
    place_row = target_row * 8 + rank_row

    early[1].wait()
    halves = parts(jnp.concatenate([pot_ref[:, :HALF], pot_ref[:, HALF:]], axis=0))

    sides = lax.div(slab + SLABS - 1, SLABS) + lax.div(2 * SLABS - 2 - slab, SLABS)
    pl.semaphore_wait(barrier, RVES - 1 + 3 * sides)

    def partner(i):
        k = lax.div(i, 2)
        step = lax.div(k + 1, 2) * (2 * lax.rem(k, 2) - 1)
        return lax.rem(my_low + 2 * step + PEERS + lax.rem(i, 2) * (1 - 2 * lax.rem(my_low, 2)), PEERS)

    def issue(t, peer_x, start, start_local):
        def one(i, carry):
            low = partner(i)
            start(low, peer_x * PEERS + low)
            return carry

        if isinstance(t, int):
            (start_local if t == 0 else start)(my_low, peer_x * PEERS + my_low)
        else:
            @pl.when(t == 0)
            def _():
                start_local(my_low, me)

            @pl.when(t > 0)
            def _():
                start(my_low, peer_x * PEERS + my_low)

        lax.fori_loop(1, PEERS, one, 0, unroll=5)

    def send(t):
        issue(
            t, lax.rem(my_x + t, GROUPS),
            lambda low, peer: pltpu.make_async_remote_copy(
                src_ref=send_phi.at[peer], dst_ref=recv_phi.at[t, my_low],
                send_sem=out_phi_send.at[t], recv_sem=out_phi_recv.at[t],
                device_id=(slab, peer), device_id_type=MESH).start(),
            lambda low, peer: pltpu.make_async_copy(
                send_phi.at[peer], recv_phi.at[t, my_low], out_phi_recv.at[t]).start())

    def send_field(t):
        issue(
            t, lax.rem(my_x + t, GROUPS),
            lambda low, peer: pltpu.make_async_remote_copy(
                src_ref=send_mac.at[peer], dst_ref=recv_mac.at[t, my_low],
                send_sem=out_mac_send.at[t], recv_sem=out_mac_recv.at[t],
                device_id=(slab, peer), device_id_type=MESH).start(),
            lambda low, peer: pltpu.make_async_copy(
                send_mac.at[peer], recv_mac.at[t, my_low], out_mac_recv.at[t]).start())

    slot_rows = iota((PEERS * 8, PTS), 0)
    for t in range(GROUPS):
        base = lax.rem(my_x + t, GROUPS) * PEERS
        rows = slot_rows + base * 8
        hot = jnp.concatenate([(rows == place_row).astype(f32), (rows == place_row + 4).astype(f32)], axis=1)
        hot = hot.astype(bf16)
        send_phi[pl.ds(base, PEERS)] = (mm(hot, halves[0], 0) + mm(hot, halves[1], 0)).reshape(PEERS, 8, HALF)
        send(t)
        if t == 0:
            early[2].wait()
            n_rows = iota((PTS, PTS), 0)
            comp = n_rows // CAP
            spread = jnp.where(comp == 0, macro_ref[0:1], jnp.where(comp == 1, macro_ref[1:2], macro_ref[2:3]))
            spread = jnp.where((comp < 3) & (n_rows % CAP == rank_row), spread, 0.0)
            owner_hot = (iota((RVES, PTS), 0) == target_row).astype(f32)
            send_mac[...] = dot_t(owner_hot, spread).reshape(RVES, 1, PTS)
            for other in range(GROUPS):
                send_field(other)
            for other in range(GROUPS):
                for copy in loads(other):
                    copy.start()
    rank_col = jnp.sum(jnp.where(same & (q_row < q_col), 1.0, 0.0), axis=1, keepdims=True).astype(jnp.int32)
    target_col = target_cols[:, :1].astype(jnp.int32)
    place_col = target_col * 8 + rank_col
    for copy in early[3:]:
        copy.wait()

    order_row = jnp.sum(jnp.where(iota((PTS, NODES), 0) == iota((PTS, NODES), 1), order_ref[...].astype(f32), 0.0),
                        axis=1, keepdims=True)
    order_cols = jnp.where(iota((PTS, PTS), 0) < NODES, jnp.broadcast_to(order_row, (PTS, PTS)), -1.0)
    order_row = order_cols.T[:1].astype(jnp.int32)
    order_col = order_cols[:ROWS].astype(jnp.int32)

    lane_peer = iota((PTS, PEERS), 0) // CAP % PEERS
    peer_t = (lane_peer == iota((PTS, PEERS), 1)).astype(f32)
    peer_m = (iota((PEERS, PTS), 1) // CAP % PEERS == iota((PEERS, PTS), 0)).astype(f32)
    mask_mac = iota((PTS, PTS), 0) % CAP == iota((PTS, PTS), 1) % CAP
    comp_m = (iota((8, PTS), 1) // CAP == iota((8, PTS), 0)).astype(f32)
    val_n = iota((PTS, 96), 0) % 32
    val_k = iota((PTS, 96), 1) // 8
    val_hot = jnp.where(
        jnp.where(val_k < 3, val_k, (val_k // 3) * 8 + val_k % 3) == val_n, 1.0 / 512.0, 0.0)
    mask_val = iota((PTS, PTS), 0) // 32 == iota((PTS, PTS), 1) % CAP

    axis2 = [[2.0 * axis_ref[c, k] for k in range(4)] for c in range(3)]
    mag_w = [[weight_ref[k] * axis_ref[c, k] for k in range(4)] for c in range(3)]
    pair_w = [[2.0 * weight_ref[k] * axis_ref[a, k] * axis_ref[b, k] for k in range(4)] for a, b in PAIRS]
    low2 = [2.0 * low_ref[k] for k in range(4)]
    high2 = [2.0 * high_ref[k] for k in range(4)]

    def evaluate(t, y, version, mean):
        now = fields[PHI + version, :, y]
        y_next = fields[PHI + version, :, lax.rem(y + 1, 8)]
        h = [mean[0] + (next_x(now) - now), mean[1] + (y_next - now), mean[2] + (next_z(now) - now)]
        g = [held[t, GRAIN + c, :, y] * h[c] for c in range(3)]
        s = []
        for k in range(4):
            arg = axis2[0][k] * g[0] + axis2[1][k] * g[1] + axis2[2][k] * g[2] - held[t, TH + k, :, y]
            s.append(jnp.tanh(arg))
        slope = [1.0 - v * v for v in s]
        perm = held[t, PERM, :, y]
        flux = []
        for c in range(3):
            mag = mag_w[c][0] * s[0] + mag_w[c][1] * s[1] + mag_w[c][2] * s[2] + mag_w[c][3] * s[3]
            flux.append(perm * h[c] + held[t, PG + c, :, y] * mag)
        stiff = {}
        for i, pair in enumerate(PAIRS):
            w = pair_w[i]
            total = w[0] * slope[0] + w[1] * slope[1] + w[2] * slope[2] + w[3] * slope[3]
            v = held[t, AIJ + i, :, y] * total
            if pair[0] == pair[1]:
                v = v + perm
            stiff[pair] = v
            stiff[pair[::-1]] = v
        return now, flux, stiff

    def sweep_body(t, y, first, mean, carry):
        now, flux, stiff = evaluate(t, y, 0 if first else 1, mean)
        if first:
            lin = stiff
        else:
            lin = {}
            psi = [fields[PSI + d, :, y] for d in range(3)]
            psi_y = [fields[PSI + d, :, lax.rem(y + 1, 8)] for d in range(3)]
            for d in range(3):
                grad = [next_x(psi[d]) - psi[d], psi_y[d] - psi[d], next_z(psi[d]) - psi[d]]
                grad[d] = grad[d] + 1.0
                for c in range(3):
                    lin[c, d] = stiff[c, 0] * grad[0] + stiff[c, 1] * grad[1] + stiff[c, 2] * grad[2]
        nxt = (flux[1], stiff[1, 1], lin[1, 0], lin[1, 1], lin[1, 2])
        cross = stiff[0, 1] + stiff[0, 2] + stiff[1, 2]
        weight = (stiff[0, 0] + stiff[1, 1] + stiff[2, 2] + (cross + cross)
                  + prev_x(stiff[0, 0]) + prev_z(stiff[2, 2]))
        force = (flux[0] - prev_x(flux[0])) + flux[1] + (flux[2] - prev_z(flux[2]))
        forces = [(lin[0, d] - prev_x(lin[0, d])) + lin[1, d] + (lin[2, d] - prev_z(lin[2, d])) for d in range(3)]
        if carry is not None:
            force, weight, forces = close(force, weight, forces, carry)
        return nxt, (force, weight, forces)

    def close(force, weight, forces, carry):
        return force - carry[0], weight + carry[1], [forces[d] - carry[2 + d] for d in range(3)]

    def apply(y, first, sums):
        force, weight, forces = sums
        inv = recip(1.5 * weight)
        old, new = (0, 1) if first else (1, 2)
        fields[PHI + new, :, y] = fields[PHI + old, :, y] + force * inv
        for d in range(3):
            step = forces[d] * inv
            if not first:
                step = fields[PSI + d, :, y] + step
            fields[PSI + (0 if first else 3) + d, :, y] = step

    def sweep(t, first, mean):
        carry, (force, weight, forces) = sweep_body(t, 0, first, mean, None)

        def step(y, carry):
            nxt, sums = sweep_body(t, y, first, mean, carry)
            apply(y, first, sums)
            return nxt

        carry = lax.fori_loop(1, 8, step, carry, unroll=UNROLL[0 if first else 1])
        apply(0, first, close(force, weight, forces, carry))

    def last(t, mean):
        def step(y, carry):
            prev, acc = carry
            now, flux, stiff = evaluate(t, y, 2, mean)
            psi = [fields[PSI + 3 + d, :, y] for d in range(3)]
            acc = list(acc)
            for c in range(3):
                acc[c] = acc[c] + sum_x(flux[c])
            for i, pair in enumerate(PAIRS):
                acc[3 + i] = acc[3 + i] + sum_x(stiff[pair])
            for c in range(3):
                div = ((stiff[0, c] - prev_x(stiff[0, c])) + (stiff[1, c] - prev[c])
                       + (stiff[2, c] - prev_z(stiff[2, c])))
                for d in range(3):
                    acc[9 + 3 * c + d] = acc[9 + 3 * c + d] + sum_x(div * psi[d])
            return (stiff[0, 1], stiff[1, 1], stiff[1, 2]), tuple(acc)

        zero = jnp.zeros((4, 8, PTS), f32)
        flat = jnp.zeros((8, PTS), f32)
        prev, acc = lax.fori_loop(0, 8, step, ((zero,) * 3, (flat,) * 18), unroll=UNROLL[2])
        psi = [fields[PSI + 3 + d, :, 0] for d in range(3)]
        for c in range(3):
            acc_ref[t, 8 * c:8 * c + 8] = acc[c]
            for d in range(3):
                pair = PAIRS.index((min(c, d), max(c, d)))
                k = 3 + 3 * c + d
                acc_ref[t, 8 * k:8 * k + 8] = acc[3 + pair] - acc[9 + 3 * c + d] + sum_x(prev[c] * psi[d])

    def turn(nat, h):
        a = nat[:, h * PTS:(h + 1) * PTS]
        b = nat[:, HALF + h * PTS:HALF + (h + 1) * PTS]
        return jnp.concatenate([a, b], axis=0).T.reshape(2, 8, 8, PTS)

    def ahead(t, carry):
        for copy in loads(t):
            copy.wait()
        for h in range(2):
            xs = slice(2 * h, 2 * h + 2)
            words_t[xs] = turn(nat_words[t], h)
            coer_t[xs] = turn(nat_coer[t], h)
            held[t, PERM, xs] = turn(nat_perm[t], h)
            for c in range(3):
                held[t, GRAIN + c, xs] = turn(nat_grain[t, c], h)

        def prepare(y, inner):
            words = words_t[:, y]
            coer = coer_t[:, y]
            for k in range(4):
                up = jnp.bitwise_and(words, 1 << k) != 0
                held[t, TH + k, :, y] = coer * jnp.where(up, low2[k], high2[k])
            perm = held[t, PERM, :, y]
            grain = [held[t, GRAIN + c, :, y] for c in range(3)]
            pg = [perm * grain[c] for c in range(3)]
            for c in range(3):
                held[t, PG + c, :, y] = pg[c]
            for i, (a, b) in enumerate(PAIRS):
                held[t, AIJ + i, :, y] = pg[a] * grain[b]
            return inner

        lax.fori_loop(0, 8, prepare, 0, unroll=UNROLL[3])
        return carry

    lax.fori_loop(0, GROUPS, ahead, 0)
    for t in range(GROUPS):
        pltpu.make_async_copy(recv_mac.at[t], recv_mac.at[t], out_mac_recv.at[t]).wait()
        mac = dot(peer_t, recv_mac[t, :, 0, :])
        means[t] = dot_t(comp_m, jnp.where(mask_mac, mac, 0.0))
    def group(t, carry):
        pltpu.make_async_copy(recv_phi.at[t], recv_phi.at[t], out_phi_recv.at[t]).wait()
        rows = to_rows(recv_phi[t])
        for h in range(2):
            fields[PHI, 2 * h:2 * h + 2] = rows[:, h * PTS:(h + 1) * PTS].T.reshape(2, 8, 8, PTS)
        mean = [jnp.broadcast_to(means[t, c:c + 1], (8, PTS))[None] for c in range(3)]

        sweep(t, True, mean)
        sweep(t, False, mean)

        first = iota((8, 8, PTS), 1) < 4
        for h in range(2):
            block = fields[PHI + 2, 2 * h:2 * h + 2].reshape(PTS, PTS).T.reshape(2, 8, 8, PTS)
            low, high = block[0], block[1]
            cols = slice(h * PTS, (h + 1) * PTS)
            ret_phi[t, :, 0, :, cols] = jnp.where(first, low, pltpu.roll(high, 4, 1))
            ret_phi[t, :, 1, :, cols] = jnp.where(first, pltpu.roll(low, 4, 1), high)

        @pl.when(t < GROUPS - HOLD)
        def _():
            give_phi(t)

        last(t, mean)
        return carry

    def give(t, src, dst, send_sem, recv_sem):
        issue(
            t, lax.rem(my_x - t + GROUPS, GROUPS),
            lambda low, peer: pltpu.make_async_remote_copy(
                src_ref=src(low), dst_ref=dst.at[me], send_sem=send_sem.at[t], recv_sem=recv_sem.at[t],
                device_id=(slab, peer), device_id_type=MESH).start(),
            lambda low, peer: pltpu.make_async_copy(src(low), dst.at[me], recv_sem.at[t]).start())

    def give_phi(t):
        give(t, lambda low: ret_phi.at[t, lax.div(low, 2), lax.rem(low, 2)], back_phi, ret_phi_send, ret_phi_recv)

    lax.fori_loop(0, GROUPS, group, 0)
    for t in range(GROUPS):
        val = jnp.where(mask_val, dot(val_hot, acc_ref[t]), 0.0)
        ret_val[t] = dot_t(peer_m, val).reshape(PEERS, 1, PTS)
    for t in range(GROUPS):
        give(t, lambda low, t=t: ret_val.at[t, low], back_val, ret_val_send, ret_val_recv)
    for t in range(GROUPS - HOLD, GROUPS):
        give_phi(t)

    for t in range(GROUPS):
        mine = back_val.at[pl.ds(lax.rem(my_x + t, GROUPS) * PEERS, PEERS)]
        pltpu.make_async_copy(mine, mine, ret_val_recv.at[t]).wait()
    owner_col = (iota((PTS, RVES), 1) == target_col).astype(f32)
    vals = dot(owner_col, back_val[:, 0, :])
    vals = jnp.where(iota((PTS, PTS), 1) // 32 == rank_col, vals, 0.0)
    fold = (iota((32, PTS), 1) % 32 == iota((32, PTS), 0)).astype(f32)
    point = dot_t(fold, vals)
    for c in range(3):
        tan_out[c] = point[8 * c + 8:8 * c + 11]

    nodal = gw_ref[0] * point[0:1] + gw_ref[1] * point[1:2] + gw_ref[2] * point[2:3]
    conn = conn_ref[...]
    spread = jnp.zeros((ROWS, PTS), f32)
    for a in range(8):
        spread = spread + jnp.where(conn[a:a + 1] == order_col, nodal[a:a + 1], 0.0)
    spread = jnp.concatenate([spread, jnp.zeros((PTS - ROWS, PTS), f32)], axis=0)
    grid = dot_t(jnp.ones((8, PTS), f32), spread)[0:1]
    halo_src[...] = grid
    turns = [(ds, dr) for ds in (-1, 0, 1) for dr in (-1, 0, 1) if (ds, dr) != (0, 0)]
    copies = [
        pltpu.make_async_remote_copy(
            src_ref=halo_src, dst_ref=halo_dst.at[i], send_sem=halo_send.at[i], recv_sem=halo_recv.at[i],
            device_id=(slab + ds, (left, me, right)[dr + 1]), device_id_type=MESH)
        for i, (ds, dr) in enumerate(turns)]
    for (ds, dr), copy in zip(turns, copies):
        toward(ds, copy.start)

    found = jnp.zeros((2 * PTS, HALF), f32)
    for t in range(GROUPS):
        base = lax.rem(my_x + t, GROUPS) * PEERS
        mine = back_phi.at[pl.ds(base, PEERS)]
        pltpu.make_async_copy(mine, mine, ret_phi_recv.at[t]).wait()
        slot_cols = iota((PTS, PEERS * 8), 1) + base * 8
        hot = jnp.concatenate([(slot_cols == place_col).astype(f32), (slot_cols == place_col + 4).astype(f32)], axis=0)
        found = found + dot(hot, mine[...].reshape(PEERS * 8, HALF))
    pot_out[:, :HALF] = found[:PTS]
    pot_out[:, HALF:] = found[PTS:]

    lane = iota((1, PTS), 1)
    at_i, at_j = lane // 15, lane // 5 % 3
    total = grid
    for i, (ds, dr) in enumerate(turns):
        toward(-ds, copies[i].wait_recv)
        ok = lane < NODES
        if dr != 0:
            ok = ok & (at_i == (0 if dr > 0 else 2)) & ((me > 0) if dr > 0 else (me < RVES - 1))
        if ds != 0:
            ok = ok & (at_j == (0 if ds > 0 else 2)) & ((slab > 0) if ds > 0 else (slab < SLABS - 1))
        shift = (-30 * dr - 10 * ds) % PTS
        moved = pltpu.roll(jnp.broadcast_to(halo_dst[i], (8, PTS)), shift, 1)[0:1]
        total = total + jnp.where(ok, moved, 0.0)
    total = jnp.where(lane < NODES, total, 0.0)
    high, low = parts(jnp.broadcast_to(total, (8, PTS)))
    node_hot = (iota((ROWS, PTS), 0) == order_row).astype(bf16)
    back = mm(high, node_hot, 1) + mm(low, node_hot, 1)
    res_out[...] = back[0:1, :NODES]

    for (ds, dr), copy in zip(turns, copies):
        toward(ds, copy.wait_send)
    for t in range(GROUPS):
        n = PEERS - 1 if t == 0 else PEERS
        pltpu.make_async_copy(send_phi.at[pl.ds(0, n)], send_phi.at[pl.ds(0, n)], out_phi_send.at[t]).wait()
        pltpu.make_async_copy(send_mac.at[pl.ds(0, n)], send_mac.at[pl.ds(0, n)], out_mac_send.at[t]).wait()
        pltpu.make_async_copy(send_phi.at[pl.ds(0, n)], send_phi.at[pl.ds(0, n)], ret_phi_send.at[t]).wait()
        pltpu.make_async_copy(send_mac.at[pl.ds(0, n)], send_mac.at[pl.ds(0, n)], ret_val_send.at[t]).wait()


def on_device(
    macro_field, rve_owner, potential, switch_words, permeability, coercivity, grain_axes,
    hyst_axis, hyst_low, hyst_high, hyst_weight, grad_weights, connectivity, node_order,
):
    vmem = pl.BlockSpec(memory_space=pltpu.VMEM)
    hbm = pl.BlockSpec(memory_space=pltpu.HBM)
    pot, tan, res = pl.pallas_call(
        kernel,
        out_shape=(
            pltpu.VMEM((PTS, 2 * HALF), f32),
            pltpu.VMEM((3, 3, PTS), f32),
            pltpu.VMEM((1, NODES), f32),
        ),
        in_specs=[hbm] * 14,
        out_specs=(vmem, vmem, vmem),
        scratch_shapes=[
            pltpu.VMEM((1, PTS), jnp.int32),
            pltpu.VMEM((3, PTS), f32),
            pltpu.VMEM((PTS, 2 * HALF), f32),
            pltpu.SMEM((3, 4), f32),
            pltpu.SMEM((4,), f32),
            pltpu.SMEM((4,), f32),
            pltpu.SMEM((4,), f32),
            pltpu.VMEM((3, 8, PTS), f32),
            pltpu.VMEM((8, PTS), jnp.int32),
            pltpu.VMEM((1, NODES), jnp.int32),
            pltpu.SemaphoreType.DMA((10,)),
            pltpu.VMEM((GROUPS, SLOTS, 2 * HALF), jnp.int32),
            pltpu.VMEM((GROUPS, SLOTS, 2 * HALF), f32),
            pltpu.VMEM((GROUPS, SLOTS, 2 * HALF), f32),
            pltpu.VMEM((GROUPS, 3, SLOTS, 2 * HALF), f32),
            pltpu.VMEM((4, 8, 8, PTS), jnp.int32),
            pltpu.VMEM((4, 8, 8, PTS), f32),
            pltpu.VMEM((GROUPS, N_HELD, 4, 8, 8, PTS), f32),
            pltpu.VMEM((N_FIELDS, 4, 8, 8, PTS), f32),
            pltpu.VMEM((RVES, 8, HALF), f32),
            pltpu.VMEM((RVES, 1, PTS), f32),
            pltpu.VMEM((GROUPS, PEERS, 8, HALF), f32),
            pltpu.VMEM((GROUPS, PEERS, 1, PTS), f32),
            pltpu.VMEM((GROUPS, PEERS // 2, 2, 8, HALF), f32),
            pltpu.VMEM((GROUPS, PEERS, 1, PTS), f32),
            pltpu.VMEM((RVES, 8, HALF), f32),
            pltpu.VMEM((RVES, 1, PTS), f32),
            pltpu.VMEM((GROUPS, 96, PTS), f32),
            pltpu.VMEM((GROUPS, 8, PTS), f32),
            pltpu.VMEM((1, PTS), f32),
            pltpu.VMEM((8, 1, PTS), f32),
            pltpu.SemaphoreType.DMA((4, GROUPS)),
        ] + [pltpu.SemaphoreType.DMA((GROUPS,))] * 8 + [pltpu.SemaphoreType.DMA((8,))] * 2,
        compiler_params=pltpu.CompilerParams(
            collective_id=0, has_side_effects=True, vmem_limit_bytes=60 * 1024 * 1024),
    )(rve_owner.reshape(1, PTS), macro_field, potential, switch_words, permeability, coercivity, grain_axes,
      hyst_axis, hyst_low, hyst_high, hyst_weight, grad_weights, connectivity, node_order.reshape(1, NODES))
    return pot, tan, res.reshape(NODES)


def solution(mesh):
    return jax.shard_map(
        on_device,
        mesh=mesh,
        in_specs=(
            P(None, ("slab", "rve")),
            P(("slab", "rve"), None),
            P(("slab", "rve"), None),
            P(("slab", "rve"), None),
            P(("slab", "rve"), None),
            P(("slab", "rve"), None),
            P(None, ("slab", "rve"), None),
            P(),
            P(),
            P(),
            P(),
            P(None, None, ("slab", "rve")),
            P(None, ("slab", "rve")),
            P(("slab", "rve")),
        ),
        out_specs=(P(("slab", "rve"), None), P(None, None, ("slab", "rve")), P(("slab", "rve"))),
        check_vma=False,
    )
```
